32 devices in a mesh: dp: 4 (over y, x), expert: 4 (over z), tensor: 2 (over core).
Axes of the slice: x: 2, y: 2, z: 4, core: 2. Of those that a mesh axis runs over, the one named last changes fastest.
Arguments:
- tokens: bfloat16 [512, 6144], P('expert'), may hold values from -6 to 6
- routes: int32 [512, 2], P('expert'), may hold values from 0 to 3, all different within a row; in each aligned block of 128 rows (0 to 127, 128 to 255, ...) at most 128 rows name the same one
- logits: float32 [512, 2], P('expert'), may hold values from -8 to 8
- grad_out: bfloat16 [512, 6144], P('expert'), may hold values from -6 to 6
- w_gate: bfloat16 [4, 6144, 8192], P('expert', None, ('dp', 'tensor')), may hold values from -0.078125 to 0.078125
- w_up: bfloat16 [4, 6144, 8192], P('expert', None, ('dp', 'tensor')), may hold values from -0.078125 to 0.078125
- w_down: bfloat16 [4, 8192, 6144], P('expert', ('dp', 'tensor')), may hold values from -0.0625 to 0.0625
Outputs:
- output: bfloat16 [512, 6144], P(('expert', 'tensor'))
- grad_tokens: bfloat16 [512, 6144], P(('expert', 'tensor'))
The draws below stay inside these ranges and needn't reach their ends.
Inputs may be any that keep to these rules, and one draw needn't show every extreme that they name: `routes`: each token names two different experts. The 128 tokens of one index of the expert axis name one expert at most 128 times, and in every draw some expert is named exactly 128 times by the tokens of some index.
All inputs are finite; a program needn't handle non-finite values.
Results may differ from the reference program's by a relative error of at most 0.015.
Values may be sent and summed in bfloat16 or wider, within the bound.
A program may use at most 128 MiB of HBM per device.

```python
import math
import jax
import jax.numpy as jnp
import numpy as np
from jax import lax

D = 6144
FFW = 8192
TOK_DEV = 128
EXPERTS = 4
CAP = 128
TOKENS = 512
N_DP = 4
N_TENSOR = 2


def steps_of(own_key, dims, pieces, least, top_value):
    gain = 1.0
    for position, blocks in pieces:
        heights = jax.random.uniform(jax.random.fold_in(jax.random.fold_in(own_key, 6), position), (blocks,), jnp.float32, least / len(pieces), top_value / len(pieces))
        gain = gain * jnp.repeat(jnp.exp(heights), dims[position] // blocks).reshape((-1,) + (1,) * (len(dims) - 1 - position))
    return gain


def assign_block(own_key, own, number, rows, number_of, top, limit, lean):
    ranking = jax.random.permutation(own_key, number_of)
    packed, ordinary = load_shares(number_of, rows * top, limit, lean, True), load_shares(number_of, rows * top, limit, lean, False)
    places = jnp.arange(number_of)

    def named(tallies, rotation):
        used = int((tallies > 0).sum())
        fixed = max(1, used // 4)
        passed = fixed + (places - fixed + rotation * (used - fixed)) % max(1, number_of - fixed)
        return jnp.zeros((number_of,), jnp.int32).at[ranking[jnp.where(places < fixed, places, passed)]].set(jnp.asarray(tallies, jnp.int32))

    tallies = jnp.where(number % 4 == 0, named(packed, number // 4), named(ordinary, number - number // 4 - 1))
    mixed = jax.random.permutation(jax.random.fold_in(own, 3), number_of)
    giver, sink = mixed[0:number_of // 2 * 2:2], mixed[1:number_of // 2 * 2:2]
    margin = jnp.minimum(tallies[giver] - 1, limit - tallies[sink]) // 2
    margin = jnp.where((giver == ranking[0]) | (sink == ranking[0]) | (tallies[sink] == 0), 0, jnp.maximum(margin, 0))
    passed = jax.random.randint(jax.random.fold_in(own, 4), (number_of // 2,), 0, 1 << 20) % (margin + 1)
    tallies = tallies.at[giver].add(-passed).at[sink].add(passed)
    members = jnp.searchsorted(jnp.cumsum(tallies), jnp.arange(rows * top), side="right").astype(jnp.int32)
    grid = members.reshape(top, rows).T
    grid = grid[jax.random.permutation(jax.random.fold_in(own, 1), rows)]
    rotation = jax.random.randint(jax.random.fold_in(own, 2), (rows, 1), 0, top)
    return jnp.take_along_axis(grid, (jnp.arange(top)[None, :] + rotation) % top, axis=1)


def load_shares(number_of, total, bound, skew, full):
    weights = [(1 << 20) // math.isqrt(grade ** skew) + 1 for grade in range(1, number_of + 1)]
    largest = bound if full else min(bound, max(-(-total // number_of), total * weights[0] // sum(weights)))
    least = 1 if total - largest >= number_of - 1 else 0
    given, spare = [largest] + [least] * (number_of - 1), total - largest - least * (number_of - 1)
    while spare > 0:
        candidates = [i for i in range(1, number_of) if given[i] < largest] or [i for i in range(1, number_of) if given[i] < bound]
        whole, budget = sum([weights[i] for i in candidates]), spare
        for i in candidates:
            more = min(bound - given[i], max(1, budget * weights[i] // whole), spare)
            given[i] = given[i] + more
            spare = spare - more
    return np.array(given)


def centred(own_key, shape, scale, most, shards=(), kind=jnp.bfloat16):
    result = jax.random.normal(own_key, shape, jnp.float32) * scale
    if len(shards) > 0:
        result = steps_of(own_key, shape, shards, -0.22, 0.18) * result
    return jnp.clip(result, min=-most, max=most).astype(kind)


def setup_inputs(seed: int = 0) -> dict:
    key_list = jax.random.split(jax.random.key(seed), 8)
    tokens = centred(key_list[0], (TOKENS, D), 1.0, 6.0, ((0, 4),))
    routes_keys = jax.random.split(jax.random.fold_in(key_list[1], 1), TOKENS // TOK_DEV)
    routes_turns = jax.random.permutation(jax.random.fold_in(key_list[1], 3), TOKENS // TOK_DEV)
    routes = jax.vmap(lambda own, number: assign_block(jax.random.fold_in(key_list[1], 2), own, number, TOK_DEV, EXPERTS, 2, CAP, 2))(routes_keys, routes_turns).reshape((TOKENS, 2))
    logits = centred(key_list[2], (TOKENS, 2), 2.0, 8.0, ((0, 4),), jnp.float32)
    grad_out = centred(key_list[3], (TOKENS, D), 1.0, 6.0, ((0, 4),))
    w_gate = centred(key_list[4], (EXPERTS, D, FFW), D ** -0.5, 0.078125, ((0, 4), (2, 8)))
    w_up = centred(key_list[5], (EXPERTS, D, FFW), D ** -0.5, 0.078125, ((0, 4), (2, 8)))
    w_down = centred(key_list[6], (EXPERTS, FFW, D), FFW ** -0.5, 0.0625, ((0, 4), (1, 8)))
    return dict(tokens=tokens, routes=routes, logits=logits, grad_out=grad_out, w_gate=w_gate, w_up=w_up, w_down=w_down)


def activate(gate, up):
    sig = jax.nn.sigmoid(gate)
    return (gate * sig * up).astype(jnp.bfloat16)


def backprop(grad_hidden, gate, up):
    sig = jax.nn.sigmoid(gate)
    grad_gate = (grad_hidden * up * sig * (1.0 + gate * (1.0 - sig))).astype(jnp.bfloat16)
    grad_up = (grad_hidden * gate * sig).astype(jnp.bfloat16)
    return grad_gate, grad_up


def round_term(term):
    narrow = lax.optimization_barrier(term.astype(jnp.bfloat16))
    return narrow.astype(jnp.float32)


def reference(tokens, routes, logits, grad_out, w_gate, w_up, w_down):
    total = tokens.shape[0]
    width = tokens.shape[1]
    blocks = N_DP * N_TENSOR
    span = w_gate.shape[2] // blocks
    most = EXPERTS * CAP
    contract_last = (((1,), (1,)), ((), ()))
    share = jax.nn.sigmoid(logits[:, 0] - logits[:, 1])
    weights = jnp.stack([share, 1.0 - share], axis=1).reshape(-1)
    flat = routes.reshape(-1).astype(jnp.int32)
    owner = jnp.arange(2 * total, dtype=jnp.int32) // 2
    order = jnp.argsort(flat, stable=True).astype(jnp.int32)
    order = jnp.concatenate([order, jnp.zeros((most,), jnp.int32)])
    labels = jnp.arange(EXPERTS, dtype=jnp.int32)
    counts = jnp.sum((flat[:, None] == labels[None, :]).astype(jnp.int32), axis=0)
    starts = (jnp.cumsum(counts) - counts).astype(jnp.int32)
    grad_rows = (weights[:, None] * grad_out[owner].astype(jnp.float32)).astype(jnp.bfloat16)
    positions = []
    valid = []
    expert_rows = []
    expert_backs = []
    for expert in range(EXPERTS):
        place = lax.dynamic_slice_in_dim(order, starts[expert], most, 0)
        positions.append(place)
        valid.append((jnp.arange(most, dtype=jnp.int32) < counts[expert])[:, None])
        expert_rows.append(tokens[owner[place]])
        expert_backs.append(grad_rows[place])

    def block_step(index, carry):
        out_total, back_total = carry
        out_terms = jnp.zeros((2 * total, width), jnp.float32)
        back_terms = jnp.zeros((2 * total, width), jnp.float32)
        for expert in range(EXPERTS):
            cols_gate = lax.dynamic_slice_in_dim(w_gate[expert], index * span, span, 1)
            cols_up = lax.dynamic_slice_in_dim(w_up[expert], index * span, span, 1)
            rows_down = lax.dynamic_slice_in_dim(w_down[expert], index * span, span, 0)
            gate = jnp.dot(expert_rows[expert], cols_gate, preferred_element_type=jnp.float32)
            up = jnp.dot(expert_rows[expert], cols_up, preferred_element_type=jnp.float32)
            hidden = activate(gate, up)
            term = round_term(jnp.dot(hidden, rows_down, preferred_element_type=jnp.float32))
            out_terms = out_terms.at[positions[expert]].add(jnp.where(valid[expert], term, 0.0))
            grad_hidden = lax.dot_general(expert_backs[expert], rows_down, contract_last, preferred_element_type=jnp.float32)
            grad_gate, grad_up = backprop(grad_hidden, gate, up)
            term_back = lax.dot_general(grad_gate, cols_gate, contract_last, preferred_element_type=jnp.float32)
            term_back = term_back + lax.dot_general(grad_up, cols_up, contract_last, preferred_element_type=jnp.float32)
            back_terms = back_terms.at[positions[expert]].add(jnp.where(valid[expert], round_term(term_back), 0.0))
        pairs = out_terms.reshape(total, 2, width)
        mixed = round_term(share[:, None] * pairs[:, 0] + (1.0 - share)[:, None] * pairs[:, 1])
        back_pairs = back_terms.reshape(total, 2, width)
        summed = round_term(back_pairs[:, 0] + back_pairs[:, 1])
        return out_total + mixed, back_total + summed

    zero = jnp.zeros((total, width), jnp.float32)
    out_total, back_total = lax.fori_loop(0, blocks, block_step, (zero, zero))
    return out_total.astype(jnp.bfloat16), back_total.astype(jnp.bfloat16)
```

```python
import functools

import jax
import jax.numpy as jnp
from jax import lax
from jax.experimental import pallas as pl
from jax.experimental.pallas import tpu as pltpu
from jax.sharding import PartitionSpec as P

MESH = pl.DeviceIdType.MESH
CONTRACT_LAST = (((1,), (1,)), ((), ()))
TILE = 256


def flip(index, mask):
    out = index
    bit = 1
    while bit <= mask:
        if mask & bit:
            out = out + bit - 2 * bit * lax.rem(index // bit, 2)
        bit *= 2
    return out


def expert_kernel(
    sizes,
    tokens,
    grads,
    table,
    w_gate,
    w_up,
    w_down,
    out_hbm,
    back_hbm,
    x_buf,
    g_buf,
    wg_buf,
    wu_buf,
    wd_buf,
    gate,
    up,
    gh,
    hid,
    gu,
    share_rows,
    share_cols,
    pair_buf,
    plane_buf,
    axis_buf,
    final_buf,
    w_sem,
    own_sem,
    t_send,
    t_recv,
    d1_send,
    d1_recv,
    d2_send,
    d2_recv,
    d3_send,
    d3_recv,
    r1_send,
    r1_recv,
    r2_send,
    r2_recv,
    r3_send,
    r3_recv,
    r4_send,
    r4_recv,
):
    lanes, experts, tensor = sizes
    i = lax.axis_index("dp")
    z = lax.axis_index("expert")
    t = lax.axis_index("tensor")
    count, width = tokens.shape
    inner = gate.shape[1]
    total = experts * count
    rows = count // tensor
    cols = width // lanes
    tile_f = min(TILE, inner)
    bufs = (x_buf, g_buf)

    def zz(k):
        return lax.rem(z + k, experts)

    def tt(s):
        return lax.rem(t + s, tensor)

    def row_ds(which):
        return pl.ds(pl.multiple_of(which * rows, rows), rows)

    def col_ds(which):
        return pl.ds(pl.multiple_of(which * cols, cols), cols)

    def remote(src, dst, send, recv, axis, target):
        return pltpu.make_async_remote_copy(
            src_ref=src,
            dst_ref=dst,
            send_sem=send,
            recv_sem=recv,
            device_id={axis: target},
            device_id_type=MESH,
        )

    def load(kind, m, slot):
        block = col_ds(flip(i, m))
        if kind == 0:
            pair = (w_gate.at[block, :], wg_buf.at[slot])
        elif kind == 1:
            pair = (w_up.at[block, :], wu_buf.at[slot])
        else:
            pair = (w_down.at[:, block], wd_buf.at[slot])
        return pltpu.make_async_copy(*pair, w_sem.at[kind, slot])

    loads = {}

    def fetch(kind, m, slot):
        loads[kind, slot] = load(kind, m, slot)
        loads[kind, slot].start()

    def fetched(kind, slot):
        copy = loads.pop((kind, slot), None)
        if copy is not None:
            copy.wait()

    own = [
        pltpu.make_async_copy(tokens, x_buf.at[z], own_sem.at[0]),
        pltpu.make_async_copy(grads, g_buf.at[z], own_sem.at[1]),
        pltpu.make_async_copy(table.at[z], share_rows.at[z], own_sem.at[2]),
    ]

    barrier = pltpu.get_barrier_semaphore()
    for k in range(1, experts):
        pl.semaphore_signal(barrier, inc=1, device_id={"expert": zz(k)}, device_id_type=MESH)
    for m in range(1, lanes):
        pl.semaphore_signal(barrier, inc=1, device_id={"dp": flip(i, m)}, device_id_type=MESH)
    for s in range(1, tensor):
        pl.semaphore_signal(barrier, inc=1, device_id={"tensor": tt(s)}, device_id_type=MESH)
    pl.semaphore_wait(barrier, experts + lanes + tensor - 3)

    def step_one(a):
        copies = []
        source = (tokens, grads)[a]
        for k in range(1, experts):
            copies.append(
                remote(
                    source.at[row_ds(t), col_ds(i)],
                    bufs[a].at[z, row_ds(t), col_ds(i)],
                    d1_send.at[a, k],
                    d1_recv.at[a, k],
                    "expert",
                    zz(k),
                )
            )
        for copy in copies:
            copy.start()
        return copies

    def step_two(a, k):
        copies = []
        place = bufs[a].at[zz(experts - k), row_ds(t), col_ds(i)]
        for m in range(1, lanes):
            copies.append(
                remote(place, place, d2_send.at[a, k, m], d2_recv.at[a, k, m], "dp", flip(i, m))
            )
        for copy in copies:
            copy.start()
        return copies

    def step_three(a, k, m):
        copies = []
        place = bufs[a].at[zz(experts - k), row_ds(t), col_ds(flip(i, m))]
        for s in range(1, tensor):
            copies.append(
                remote(
                    place, place, d3_send.at[a, k, m, s], d3_recv.at[a, k, m, s], "tensor", tt(s)
                )
            )
        for copy in copies:
            copy.start()
        return copies

    first = {0: step_one(0)}
    shares = []
    for k in range(1, experts):
        shares.append(
            remote(
                table.at[zz(k)],
                share_rows.at[z],
                t_send.at[k],
                t_recv.at[k],
                "expert",
                zz(k),
            )
        )
    for copy in shares:
        copy.start()
    for copy in own:
        copy.start()
    for slot in range(2):
        fetch(0, slot, slot)
        fetch(1, slot, slot)
    for slot in range(2):
        fetch(2, lanes - 1 - slot, slot)

    second = {}
    third = {}

    def relay_one(a):
        for k in range(1, experts):
            first[a][k - 1].wait_recv()
            second[a, k] = step_two(a, k)
            third[a, k, 0] = step_three(a, k, 0)

    def relay_two(a, m):
        for k in range(1, experts):
            second[a, k][m - 1].wait_recv()
            third[a, k, m] = step_three(a, k, m)

    def arrived(a, m):
        for k in range(1, experts):
            for copy in third[a, k, m]:
                copy.wait_recv()

    def sent(a):
        for copy in first[a]:
            copy.wait_send()
        for k in range(1, experts):
            for copy in second[a, k]:
                copy.wait_send()
            for m in range(lanes):
                for copy in third[a, k, m]:
                    copy.wait_send()

    def operand(a, m):
        return bufs[a][:, :, col_ds(flip(i, m))].reshape(total, cols)

    relay_one(0)
    first[1] = step_one(1)
    own[0].wait()
    for m in range(lanes):
        if m + 1 < lanes:
            relay_two(0, m + 1)
        else:
            relay_one(1)
        arrived(0, m)
        slot = m % 2
        fetched(0, slot)
        fetched(1, slot)

        def project(n, carry, m=m, slot=slot):
            span = pl.ds(pl.multiple_of(n * tile_f, tile_f), tile_f)
            left = operand(0, m)
            one = jnp.dot(left, wg_buf[slot, :, span], preferred_element_type=jnp.float32)
            two = jnp.dot(left, wu_buf[slot, :, span], preferred_element_type=jnp.float32)
            if m == 0:
                gate[:, span] = one
                up[:, span] = two
            else:
                gate[:, span] += one
                up[:, span] += two
            return carry

        lax.fori_loop(0, inner // tile_f, project, 0)
        if m + 2 < lanes:
            fetch(0, m + 2, slot)
            fetch(1, m + 2, slot)

    own[2].wait()
    for copy in shares:
        copy.wait()
    for e in range(experts):
        share_cols[e * count : (e + 1) * count, :] = jnp.broadcast_to(
            share_rows[e, 0:1, :], (count, count)
        ).T

    def activate(e, carry):
        span = pl.ds(pl.multiple_of(e * count, count), count)
        weight = share_cols[span, 0:1]
        for f in range(0, inner, tile_f):
            v = gate[span, f : f + tile_f]
            sig = jax.nn.sigmoid(v)
            hid[span, f : f + tile_f] = (v * sig * up[span, f : f + tile_f] * weight).astype(
                jnp.bfloat16
            )
        return carry

    lax.fori_loop(0, experts, activate, 0)
    sent(0)

    pairs = {}
    planes = {}

    def pair_send(a, m):
        copies = []
        for s in range(1, tensor):
            copies.append(
                remote(
                    bufs[a].at[:, row_ds(tt(s)), col_ds(flip(i, m))],
                    pair_buf.at[a, m, s - 1],
                    r1_send.at[a, m, s],
                    r1_recv.at[a, m, s],
                    "tensor",
                    tt(s),
                )
            )
        for copy in copies:
            copy.start()
        pairs[a, m] = copies

    def pair_sum(a, m):
        for copy in pairs[a, m]:
            copy.wait_recv()
        block = col_ds(flip(i, m))

        def add(e, carry):
            value = bufs[a][e, row_ds(t), block].astype(jnp.float32)
            for s in range(tensor - 1):
                value = value + pair_buf[a, m, s, e].astype(jnp.float32)
            bufs[a][e, row_ds(t), block] = value.astype(jnp.bfloat16)
            return carry

        lax.fori_loop(0, experts, add, 0)
        if m == 0:
            return
        for k in list(range(1, experts)) + [0]:
            copy = remote(
                bufs[a].at[zz(k), row_ds(t), block],
                plane_buf.at[a, m - 1, zz(k)],
                r2_send.at[a, m, k],
                r2_recv.at[a, m, k],
                "dp",
                flip(i, m),
            )
            copy.start()
            planes[a, m, k] = copy

    for n in range(lanes):
        m = lanes - 1 - n
        slot = n % 2
        fetched(2, slot)

        def down(c, carry, m=m, slot=slot):
            span = pl.ds(pl.multiple_of(c * TILE, TILE), TILE)
            to = pl.ds(pl.multiple_of(flip(i, m) * cols + c * TILE, TILE), TILE)
            value = jnp.dot(hid[...], wd_buf[slot, :, span], preferred_element_type=jnp.float32)
            x_buf[:, :, to] = value.astype(jnp.bfloat16).reshape(experts, count, TILE)
            return carry

        lax.fori_loop(0, cols // TILE, down, 0)
        if n + 2 < lanes:
            fetch(2, lanes - 1 - (n + 2), slot)
        pair_send(0, m)
        if n > 0:
            pair_sum(0, m + 1)
    relay_two(1, 1)
    pair_sum(0, 0)

    own[1].wait()
    for m in range(lanes):
        if 1 <= m < lanes - 1:
            relay_two(1, m + 1)
        arrived(1, m)
        slot = (lanes - 1 - m) % 2
        fetched(2, slot)

        def project_back(n, carry, m=m, slot=slot):
            span = pl.ds(pl.multiple_of(n * tile_f, tile_f), tile_f)
            value = lax.dot_general(
                operand(1, m),
                wd_buf[slot, span, :],
                CONTRACT_LAST,
                preferred_element_type=jnp.float32,
            )
            if m == 0:
                gh[:, span] = value
            else:
                gh[:, span] += value
            return carry

        lax.fori_loop(0, inner // tile_f, project_back, 0)
        if m + 2 < lanes:
            fetch(2, m + 2, slot)

    def differentiate(e, carry):
        span = pl.ds(pl.multiple_of(e * count, count), count)
        weight = share_cols[span, 0:1]
        for f in range(0, inner, tile_f):
            part = slice(f, f + tile_f)
            v = gate[span, part]
            sig = jax.nn.sigmoid(v)
            slope = gh[span, part] * weight * sig
            hid[span, part] = (slope * up[span, part] * (1.0 + v * (1.0 - sig))).astype(
                jnp.bfloat16
            )
            gu[span, part] = (slope * v).astype(jnp.bfloat16)
        return carry

    lax.fori_loop(0, experts, differentiate, 0)
    sent(1)

    for n in range(lanes):
        m = lanes - 1 - n
        slot = m % 2
        fetched(0, slot)
        fetched(1, slot)

        def back(c, carry, m=m, slot=slot):
            span = pl.ds(pl.multiple_of(c * TILE, TILE), TILE)
            to = pl.ds(pl.multiple_of(flip(i, m) * cols + c * TILE, TILE), TILE)
            value = lax.dot_general(
                hid[...], wg_buf[slot, span, :], CONTRACT_LAST, preferred_element_type=jnp.float32
            )
            value = value + lax.dot_general(
                gu[...], wu_buf[slot, span, :], CONTRACT_LAST, preferred_element_type=jnp.float32
            )
            g_buf[:, :, to] = value.astype(jnp.bfloat16).reshape(experts, count, TILE)
            return carry

        lax.fori_loop(0, cols // TILE, back, 0)
        if n + 2 < lanes:
            fetch(0, m - 2, slot)
            fetch(1, m - 2, slot)
        pair_send(1, m)
        if n > 0:
            pair_sum(1, m + 1)
    pair_sum(1, 0)

    crossing = {}
    for a in range(2):
        for k in list(range(1, experts)) + [0]:
            for m in range(1, lanes):
                planes[a, m, k].wait_recv()
            place = bufs[a].at[zz(k), row_ds(t), col_ds(i)]
            value = place[...].astype(jnp.float32)
            for m in range(1, lanes):
                value = value + plane_buf[a, m - 1, zz(k)].astype(jnp.float32)
            place[...] = value.astype(jnp.bfloat16)
            if k > 0:
                copy = remote(
                    place,
                    axis_buf.at[a, k - 1],
                    r3_send.at[a, k],
                    r3_recv.at[a, k],
                    "expert",
                    zz(k),
                )
                copy.start()
                crossing[a, k] = copy
    finals = []
    for a in range(2):
        value = bufs[a][z, row_ds(t), col_ds(i)].astype(jnp.float32)
        for k in range(1, experts):
            crossing[a, k].wait_recv()
            value = value + axis_buf[a, k - 1].astype(jnp.float32)
        final_buf[a] = value.astype(jnp.bfloat16)
        target = (out_hbm, back_hbm)[a].at[:, col_ds(i)]
        for m in range(1, lanes):
            finals.append(
                remote(
                    final_buf.at[a], target, r4_send.at[a, m], r4_recv.at[a, m], "dp", flip(i, m)
                )
            )
        finals.append(pltpu.make_async_copy(final_buf.at[a], target, own_sem.at[3 + a]))
        for copy in finals[-lanes:]:
            copy.start()
    for copies in pairs.values():
        for copy in copies:
            copy.wait_send()
    for copy in planes.values():
        copy.wait_send()
    for copy in crossing.values():
        copy.wait_send()
    for copy in finals:
        copy.wait()


def local(sizes, tokens, routes, logits, grad_out, w_gate, w_up, w_down):
    lanes, experts, tensor = sizes
    count, width = tokens.shape
    inner = w_gate.shape[2]
    rows = count // tensor
    cols = width // lanes
    total = experts * count
    share = jax.nn.sigmoid(logits[:, 0] - logits[:, 1])
    labels = jnp.arange(experts, dtype=jnp.int32)[:, None]
    table = jnp.where(routes[None, :, 0] == labels, share[None, :], 0.0)
    table = table + jnp.where(routes[None, :, 1] == labels, 1.0 - share[None, :], 0.0)
    table = jnp.broadcast_to(table[:, None, :], (experts, 8, count))
    bf16 = jnp.bfloat16
    f32 = jnp.float32
    dma = pltpu.SemaphoreType.DMA
    result = jax.ShapeDtypeStruct((rows, width), bf16)
    anywhere = pl.BlockSpec(memory_space=pl.ANY)
    flops = 2 * total * width * inner * 6
    return pl.pallas_call(
        functools.partial(expert_kernel, sizes),
        out_shape=(result, result),
        in_specs=[anywhere] * 6,
        out_specs=(anywhere, anywhere),
        scratch_shapes=[
            pltpu.VMEM((experts, count, width), bf16),
            pltpu.VMEM((experts, count, width), bf16),
            pltpu.VMEM((2, cols, inner), bf16),
            pltpu.VMEM((2, cols, inner), bf16),
            pltpu.VMEM((2, inner, cols), bf16),
            pltpu.VMEM((total, inner), f32),
            pltpu.VMEM((total, inner), f32),
            pltpu.VMEM((total, inner), f32),
            pltpu.VMEM((total, inner), bf16),
            pltpu.VMEM((total, inner), bf16),
            pltpu.VMEM((experts, 8, count), f32),
            pltpu.VMEM((total, count), f32),
            pltpu.VMEM((2, lanes, tensor - 1, experts, rows, cols), bf16),
            pltpu.VMEM((2, lanes - 1, experts, rows, cols), bf16),
            pltpu.VMEM((2, experts - 1, rows, cols), bf16),
            pltpu.VMEM((2, rows, cols), bf16),
            dma((3, 2)),
            dma((5,)),
            dma((experts,)),
            dma((experts,)),
            dma((2, experts)),
            dma((2, experts)),
            dma((2, experts, lanes)),
            dma((2, experts, lanes)),
            dma((2, experts, lanes, tensor)),
            dma((2, experts, lanes, tensor)),
            dma((2, lanes, tensor)),
            dma((2, lanes, tensor)),
            dma((2, lanes, experts)),
            dma((2, lanes, experts)),
            dma((2, experts)),
            dma((2, experts)),
            dma((2, lanes)),
            dma((2, lanes)),
        ],
        compiler_params=pltpu.CompilerParams(
            collective_id=0, has_side_effects=True, vmem_limit_bytes=62 * 1024 * 1024
        ),
        cost_estimate=pl.CostEstimate(
            flops=flops, bytes_accessed=6 * width * inner * 2, transcendentals=2 * total * inner
        ),
        name="expert_layer",
    )(tokens, grad_out, table, w_gate[0], w_up[0], w_down[0])


def solution(mesh):
    sizes = (mesh.shape["dp"], mesh.shape["expert"], mesh.shape["tensor"])
    return jax.shard_map(
        functools.partial(local, sizes),
        mesh=mesh,
        in_specs=(
            P("expert", None),
            P("expert", None),
            P("expert", None),
            P("expert", None),
            P("expert", None, ("dp", "tensor")),
            P("expert", None, ("dp", "tensor")),
            P("expert", ("dp", "tensor"), None),
        ),
        out_specs=(P(("expert", "tensor"), None), P(("expert", "tensor"), None)),
        check_vma=False,
    )
```

```python
import functools

import jax
import jax.numpy as jnp
from jax import lax
from jax.experimental import pallas as pl
from jax.experimental.pallas import tpu as pltpu
from jax.sharding import PartitionSpec as P

MESH = pl.DeviceIdType.MESH
CONTRACT_LAST = (((1,), (1,)), ((), ()))
TILE = 256


def flip(index, mask):
    out = index
    bit = 1
    while bit <= mask:
        if mask & bit:
            out = out + bit - 2 * bit * lax.rem(index // bit, 2)
        bit *= 2
    return out


def expert_kernel(
    sizes,
    tokens,
    grads,
    table,
    w_gate,
    w_up,
    w_down,
    out_hbm,
    back_hbm,
    x_buf,
    g_buf,
    wg_buf,
    wu_buf,
    wd_buf,
    gate,
    up,
    gh,
    hid,
    gu,
    share_rows,
    share_cols,
    pair_buf,
    plane_buf,
    via_buf,
    axis_buf,
    final_buf,
    w_sem,
    own_sem,
    t_send,
    t_recv,
    d1_send,
    d1_recv,
    d2_send,
    d2_recv,
    d3_send,
    d3_recv,
    r1_send,
    r1_recv,
    r2_send,
    r2_recv,
    via_send,
    via_recv,
    r3_send,
    r3_recv,
    r4_send,
    r4_recv,
):
    lanes, experts, tensor = sizes
    i = lax.axis_index("dp")
    z = lax.axis_index("expert")
    t = lax.axis_index("tensor")
    count, width = tokens.shape
    inner = gate.shape[1]
    total = experts * count
    rows = count // tensor
    cols = width // lanes
    half = cols // 2
    tile_f = min(TILE, inner)
    bufs = (x_buf, g_buf)

    def zz(k):
        return lax.rem(z + k, experts)

    def tt(s):
        return lax.rem(t + s, tensor)

    def row_ds(which):
        return pl.ds(pl.multiple_of(which * rows, rows), rows)

    def col_ds(which):
        return pl.ds(pl.multiple_of(which * cols, cols), cols)

    def half_ds(which, part):
        return pl.ds(pl.multiple_of(which * cols + part * half, half), half)

    def remote(src, dst, send, recv, axis, target):
        return pltpu.make_async_remote_copy(
            src_ref=src,
            dst_ref=dst,
            send_sem=send,
            recv_sem=recv,
            device_id={axis: target},
            device_id_type=MESH,
        )

    def load(kind, m, slot):
        block = col_ds(flip(i, m))
        if kind == 0:
            pair = (w_gate.at[block, :], wg_buf.at[slot])
        elif kind == 1:
            pair = (w_up.at[block, :], wu_buf.at[slot])
        else:
            pair = (w_down.at[:, block], wd_buf.at[slot])
        return pltpu.make_async_copy(*pair, w_sem.at[kind, slot])

    loads = {}

    def fetch(kind, m, slot):
        loads[kind, slot] = load(kind, m, slot)
        loads[kind, slot].start()

    def fetched(kind, slot):
        copy = loads.pop((kind, slot), None)
        if copy is not None:
            copy.wait()

    own = [
        pltpu.make_async_copy(tokens, x_buf.at[z], own_sem.at[0]),
        pltpu.make_async_copy(grads, g_buf.at[z], own_sem.at[1]),
        pltpu.make_async_copy(table.at[z], share_rows.at[z], own_sem.at[2]),
    ]

    barrier = pltpu.get_barrier_semaphore()
    for k in range(1, experts):
        pl.semaphore_signal(barrier, inc=1, device_id={"expert": zz(k)}, device_id_type=MESH)
    for m in range(1, lanes):
        pl.semaphore_signal(barrier, inc=1, device_id={"dp": flip(i, m)}, device_id_type=MESH)
    for s in range(1, tensor):
        pl.semaphore_signal(barrier, inc=1, device_id={"tensor": tt(s)}, device_id_type=MESH)
    pl.semaphore_wait(barrier, experts + lanes + tensor - 3)

    def step_one(a):
        copies = []
        source = (tokens, grads)[a]
        for k in range(1, experts):
            copies.append(
                remote(
                    source.at[row_ds(t), col_ds(i)],
                    bufs[a].at[z, row_ds(t), col_ds(i)],
                    d1_send.at[a, k],
                    d1_recv.at[a, k],
                    "expert",
                    zz(k),
                )
            )
        for copy in copies:
            copy.start()
        return copies

    def step_two(a, k):
        place = bufs[a].at[zz(experts - k), row_ds(t), col_ds(i)]
        for m in (1, 2):
            copy = remote(
                place, place, d2_send.at[a, k, m], d2_recv.at[a, k, m], "dp", flip(i, m)
            )
            copy.start()
            second[a, k, m] = [copy]

    def step_across(a, k, m):
        place = bufs[a].at[zz(experts - k), row_ds(t), half_ds(flip(i, m), m - 1)]
        copy = remote(
            place, place, d2_send.at[a, k, m + 2], d2_recv.at[a, k, m + 2], "dp", flip(i, 3 - m)
        )
        copy.start()
        second.setdefault((a, k, 3), []).append(copy)

    def step_three(a, k, m):
        copies = []
        place = bufs[a].at[zz(experts - k), row_ds(t), col_ds(flip(i, m))]
        for s in range(1, tensor):
            copies.append(
                remote(
                    place, place, d3_send.at[a, k, m, s], d3_recv.at[a, k, m, s], "tensor", tt(s)
                )
            )
        for copy in copies:
            copy.start()
        return copies

    first = {0: step_one(0)}
    shares = []
    for k in range(1, experts):
        shares.append(
            remote(
                table.at[zz(k)],
                share_rows.at[z],
                t_send.at[k],
                t_recv.at[k],
                "expert",
                zz(k),
            )
        )
    for copy in shares:
        copy.start()
    for copy in own:
        copy.start()
    for slot in range(2):
        fetch(0, slot, slot)
        fetch(1, slot, slot)
    for slot in range(2):
        fetch(2, lanes - 1 - slot, slot)

    second = {}
    third = {}

    def relay_one(a, k):
        first[a][k - 1].wait_recv()
        step_two(a, k)
        third[a, k, 0] = step_three(a, k, 0)

    def relay_two(a, k, m):
        for copy in second[a, k, m]:
            copy.wait_recv()
        if m < 3:
            step_across(a, k, m)
        third[a, k, m] = step_three(a, k, m)

    def arrived(a, m):
        for k in range(1, experts):
            for copy in third[a, k, m]:
                copy.wait_recv()

    def sent(a):
        for copy in first[a]:
            copy.wait_send()
        for k in range(1, experts):
            for m in range(1, lanes):
                for copy in second[a, k, m]:
                    copy.wait_send()
            for m in range(lanes):
                for copy in third[a, k, m]:
                    copy.wait_send()

    def operand(a, m):
        return bufs[a][:, :, col_ds(flip(i, m))].reshape(total, cols)

    others = list(range(1, experts))
    for k in others:
        relay_one(0, k)
    first[1] = step_one(1)
    own[0].wait()
    for m in range(lanes):
        if m + 1 < lanes:
            for k in others:
                relay_two(0, k, m + 1)
        for k in others:
            if m == min(k, lanes - 1):
                relay_one(1, k)
        arrived(0, m)
        slot = m % 2
        fetched(0, slot)
        fetched(1, slot)

        def project(n, carry, m=m, slot=slot):
            span = pl.ds(pl.multiple_of(n * tile_f, tile_f), tile_f)
            left = operand(0, m)
            one = jnp.dot(left, wg_buf[slot, :, span], preferred_element_type=jnp.float32)
            two = jnp.dot(left, wu_buf[slot, :, span], preferred_element_type=jnp.float32)
            if m == 0:
                gate[:, span] = one
                up[:, span] = two
            else:
                gate[:, span] += one
                up[:, span] += two
            return carry

        lax.fori_loop(0, inner // tile_f, project, 0)
        if m + 2 < lanes:
            fetch(0, m + 2, slot)
            fetch(1, m + 2, slot)

    own[2].wait()
    for copy in shares:
        copy.wait()
    for e in range(experts):
        share_cols[e * count : (e + 1) * count, :] = jnp.broadcast_to(
            share_rows[e, 0:1, :], (count, count)
        ).T

    def activate(e, carry):
        span = pl.ds(pl.multiple_of(e * count, count), count)
        weight = share_cols[span, 0:1]
        for f in range(0, inner, tile_f):
            v = gate[span, f : f + tile_f]
            sig = jax.nn.sigmoid(v)
            hid[span, f : f + tile_f] = (v * sig * up[span, f : f + tile_f] * weight).astype(
                jnp.bfloat16
            )
        return carry

    lax.fori_loop(0, experts, activate, 0)
    sent(0)

    pairs = {}
    planes = {}
    vias = {}
    order = others + [0]

    def pair_send(a, m):
        copies = []
        for s in range(1, tensor):
            copies.append(
                remote(
                    bufs[a].at[:, row_ds(tt(s)), col_ds(flip(i, m))],
                    pair_buf.at[a, m, s - 1],
                    r1_send.at[a, m, s],
                    r1_recv.at[a, m, s],
                    "tensor",
                    tt(s),
                )
            )
        for copy in copies:
            copy.start()
        pairs[a, m] = copies

    def pair_sum(a, m):
        for copy in pairs[a, m]:
            copy.wait_recv()
        block = col_ds(flip(i, m))

        def add(e, carry):
            value = bufs[a][e, row_ds(t), block].astype(jnp.float32)
            for s in range(tensor - 1):
                value = value + pair_buf[a, m, s, e].astype(jnp.float32)
            bufs[a][e, row_ds(t), block] = value.astype(jnp.bfloat16)
            return carry

        lax.fori_loop(0, experts, add, 0)
        for k in order:
            if m == 3:
                for part in range(2):
                    copy = remote(
                        bufs[a].at[zz(k), row_ds(t), half_ds(flip(i, 3), part)],
                        via_buf.at[a, part, zz(k)],
                        via_send.at[a, part, k],
                        via_recv.at[a, part, k],
                        "dp",
                        flip(i, part + 1),
                    )
                    copy.start()
                    vias[a, part, k] = copy
            elif m > 0:
                plane_send(a, m, k, m - 1)

    def plane_send(a, m, k, part):
        copy = remote(
            bufs[a].at[zz(k), row_ds(t), half_ds(flip(i, m), part)],
            plane_buf.at[a, m - 1, zz(k), :, part * half : (part + 1) * half],
            r2_send.at[a, m - 1, part, k],
            r2_recv.at[a, m - 1, part, k],
            "dp",
            flip(i, m),
        )
        copy.start()
        planes[a, m, part, k] = copy

    def via_sum(a):
        for k in order:
            for part in range(2):
                m = 2 - part
                vias[a, part, k].wait_recv()
                place = bufs[a].at[zz(k), row_ds(t), half_ds(flip(i, m), part)]
                value = place[...].astype(jnp.float32)
                value = value + via_buf[a, part, zz(k)].astype(jnp.float32)
                place[...] = value.astype(jnp.bfloat16)
                plane_send(a, m, k, part)

    for n in range(lanes):
        m = lanes - 1 - n
        slot = n % 2
        fetched(2, slot)

        def down(c, carry, m=m, slot=slot):
            span = pl.ds(pl.multiple_of(c * TILE, TILE), TILE)
            to = pl.ds(pl.multiple_of(flip(i, m) * cols + c * TILE, TILE), TILE)
            value = jnp.dot(hid[...], wd_buf[slot, :, span], preferred_element_type=jnp.float32)
            x_buf[:, :, to] = value.astype(jnp.bfloat16).reshape(experts, count, TILE)
            return carry

        lax.fori_loop(0, cols // TILE, down, 0)
        if n + 2 < lanes:
            fetch(2, lanes - 1 - (n + 2), slot)
        pair_send(0, m)
        if n > 0:
            pair_sum(0, m + 1)
            for k in others:
                if n == min(k, lanes - 1):
                    relay_two(1, k, 1)
                    relay_two(1, k, 2)
    pair_sum(0, 0)

    own[1].wait()
    for m in range(lanes):
        if m == lanes - 2:
            for k in others:
                relay_two(1, k, 3)
        arrived(1, m)
        slot = (lanes - 1 - m) % 2
        fetched(2, slot)

        def project_back(n, carry, m=m, slot=slot):
            span = pl.ds(pl.multiple_of(n * tile_f, tile_f), tile_f)
            value = lax.dot_general(
                operand(1, m),
                wd_buf[slot, span, :],
                CONTRACT_LAST,
                preferred_element_type=jnp.float32,
            )
            if m == 0:
                gh[:, span] = value
            else:
                gh[:, span] += value
            return carry

        lax.fori_loop(0, inner // tile_f, project_back, 0)
        if m + 2 < lanes:
            fetch(2, m + 2, slot)

    def differentiate(e, carry):
        span = pl.ds(pl.multiple_of(e * count, count), count)
        weight = share_cols[span, 0:1]
        for f in range(0, inner, tile_f):
            part = slice(f, f + tile_f)
            v = gate[span, part]
            sig = jax.nn.sigmoid(v)
            slope = gh[span, part] * weight * sig
            hid[span, part] = (slope * up[span, part] * (1.0 + v * (1.0 - sig))).astype(
                jnp.bfloat16
            )
            gu[span, part] = (slope * v).astype(jnp.bfloat16)
        return carry

    lax.fori_loop(0, experts, differentiate, 0)
    sent(1)

    for n in range(lanes):
        m = lanes - 1 - n
        slot = m % 2
        fetched(0, slot)
        fetched(1, slot)

        def back(c, carry, m=m, slot=slot):
            span = pl.ds(pl.multiple_of(c * TILE, TILE), TILE)
            to = pl.ds(pl.multiple_of(flip(i, m) * cols + c * TILE, TILE), TILE)
            value = lax.dot_general(
                hid[...], wg_buf[slot, span, :], CONTRACT_LAST, preferred_element_type=jnp.float32
            )
            value = value + lax.dot_general(
                gu[...], wu_buf[slot, span, :], CONTRACT_LAST, preferred_element_type=jnp.float32
            )
            g_buf[:, :, to] = value.astype(jnp.bfloat16).reshape(experts, count, TILE)
            return carry

        lax.fori_loop(0, cols // TILE, back, 0)
        if n + 2 < lanes:
            fetch(0, m - 2, slot)
            fetch(1, m - 2, slot)
        pair_send(1, m)
        if n == 0:
            via_sum(0)
        else:
            pair_sum(1, m + 1)
    pair_sum(1, 0)

    crossing = {}
    for a in range(2):
        if a == 1:
            via_sum(1)
        for k in order:
            for m in (1, 2):
                for part in range(2):
                    planes[a, m, part, k].wait_recv()
            place = bufs[a].at[zz(k), row_ds(t), col_ds(i)]
            value = place[...].astype(jnp.float32)
            for m in (1, 2):
                value = value + plane_buf[a, m - 1, zz(k)].astype(jnp.float32)
            place[...] = value.astype(jnp.bfloat16)
            if k > 0:
                copy = remote(
                    place,
                    axis_buf.at[a, k - 1],
                    r3_send.at[a, k],
                    r3_recv.at[a, k],
                    "expert",
                    zz(k),
                )
                copy.start()
                crossing[a, k] = copy
    finals = []
    for a in range(2):
        value = bufs[a][z, row_ds(t), col_ds(i)].astype(jnp.float32)
        for k in range(1, experts):
            crossing[a, k].wait_recv()
            value = value + axis_buf[a, k - 1].astype(jnp.float32)
        final_buf[a] = value.astype(jnp.bfloat16)
        target = (out_hbm, back_hbm)[a].at[:, col_ds(i)]
        for m in range(1, lanes):
            finals.append(
                remote(
                    final_buf.at[a], target, r4_send.at[a, m], r4_recv.at[a, m], "dp", flip(i, m)
                )
            )
        finals.append(pltpu.make_async_copy(final_buf.at[a], target, own_sem.at[3 + a]))
        for copy in finals[-lanes:]:
            copy.start()
    for copies in pairs.values():
        for copy in copies:
            copy.wait_send()
    for copy in vias.values():
        copy.wait_send()
    for copy in planes.values():
        copy.wait_send()
    for copy in crossing.values():
        copy.wait_send()
    for copy in finals:
        copy.wait()


def local(sizes, tokens, routes, logits, grad_out, w_gate, w_up, w_down):
    lanes, experts, tensor = sizes
    count, width = tokens.shape
    inner = w_gate.shape[2]
    rows = count // tensor
    cols = width // lanes
    total = experts * count
    share = jax.nn.sigmoid(logits[:, 0] - logits[:, 1])
    labels = jnp.arange(experts, dtype=jnp.int32)[:, None]
    table = jnp.where(routes[None, :, 0] == labels, share[None, :], 0.0)
    table = table + jnp.where(routes[None, :, 1] == labels, 1.0 - share[None, :], 0.0)
    table = jnp.broadcast_to(table[:, None, :], (experts, 8, count))
    bf16 = jnp.bfloat16
    f32 = jnp.float32
    dma = pltpu.SemaphoreType.DMA
    result = jax.ShapeDtypeStruct((rows, width), bf16)
    anywhere = pl.BlockSpec(memory_space=pl.ANY)
    flops = 2 * total * width * inner * 6
    return pl.pallas_call(
        functools.partial(expert_kernel, sizes),
        out_shape=(result, result),
        in_specs=[anywhere] * 6,
        out_specs=(anywhere, anywhere),
        scratch_shapes=[
            pltpu.VMEM((experts, count, width), bf16),
            pltpu.VMEM((experts, count, width), bf16),
            pltpu.VMEM((2, cols, inner), bf16),
            pltpu.VMEM((2, cols, inner), bf16),
            pltpu.VMEM((2, inner, cols), bf16),
            pltpu.VMEM((total, inner), f32),
            pltpu.VMEM((total, inner), f32),
            pltpu.VMEM((total, inner), f32),
            pltpu.VMEM((total, inner), bf16),
            pltpu.VMEM((total, inner), bf16),
            pltpu.VMEM((experts, 8, count), f32),
            pltpu.VMEM((total, count), f32),
            pltpu.VMEM((2, lanes, tensor - 1, experts, rows, cols), bf16),
            pltpu.VMEM((2, 2, experts, rows, cols), bf16),
            pltpu.VMEM((2, 2, experts, rows, cols // 2), bf16),
            pltpu.VMEM((2, experts - 1, rows, cols), bf16),
            pltpu.VMEM((2, rows, cols), bf16),
            dma((3, 2)),
            dma((5,)),
            dma((experts,)),
            dma((experts,)),
            dma((2, experts)),
            dma((2, experts)),
            dma((2, experts, 5)),
            dma((2, experts, 5)),
            dma((2, experts, lanes, tensor)),
            dma((2, experts, lanes, tensor)),
            dma((2, lanes, tensor)),
            dma((2, lanes, tensor)),
            dma((2, 2, 2, experts)),
            dma((2, 2, 2, experts)),
            dma((2, 2, experts)),
            dma((2, 2, experts)),
            dma((2, experts)),
            dma((2, experts)),
            dma((2, lanes)),
            dma((2, lanes)),
        ],
        compiler_params=pltpu.CompilerParams(
            collective_id=0, has_side_effects=True, vmem_limit_bytes=62 * 1024 * 1024
        ),
        cost_estimate=pl.CostEstimate(
            flops=flops, bytes_accessed=6 * width * inner * 2, transcendentals=2 * total * inner
        ),
        name="expert_layer",
    )(tokens, grad_out, table, w_gate[0], w_up[0], w_down[0])


def solution(mesh):
    sizes = (mesh.shape["dp"], mesh.shape["expert"], mesh.shape["tensor"])
    return jax.shard_map(
        functools.partial(local, sizes),
        mesh=mesh,
        in_specs=(
            P("expert", None),
            P("expert", None),
            P("expert", None),
            P("expert", None),
            P("expert", None, ("dp", "tensor")),
            P("expert", None, ("dp", "tensor")),
            P("expert", ("dp", "tensor"), None),
        ),
        out_specs=(P(("expert", "tensor"), None), P(("expert", "tensor"), None)),
        check_vma=False,
    )
```

```python
import functools

import jax
import jax.numpy as jnp
from jax import lax
from jax.experimental import pallas as pl
from jax.experimental.pallas import tpu as pltpu
from jax.sharding import PartitionSpec as P

MESH = pl.DeviceIdType.MESH
CONTRACT_LAST = (((1,), (1,)), ((), ()))
TILE = 512
GROUPS = (1, 2)


def flip(index, mask):
    out = index
    bit = 1
    while bit <= mask:
        if mask & bit:
            out = out + bit - 2 * bit * lax.rem(index // bit, 2)
        bit *= 2
    return out


def expert_kernel(
    sizes,
    tokens,
    grads,
    table,
    w_gate,
    w_up,
    w_down,
    out_hbm,
    back_hbm,
    x_buf,
    g_buf,
    wg_buf,
    wu_buf,
    wd_buf,
    gate,
    up,
    gh,
    hid,
    gu,
    share_rows,
    share_cols,
    pair_buf,
    plane_buf,
    via_buf,
    axis_buf,
    final_buf,
    w_sem,
    own_sem,
    t_send,
    t_recv,
    d1_send,
    d1_recv,
    d2_send,
    d2_recv,
    d3_send,
    d3_recv,
    r1_send,
    r1_recv,
    r2_send,
    r2_recv,
    via_send,
    via_recv,
    r3_send,
    r3_recv,
    r4_send,
    r4_recv,
):
    lanes, experts, tensor = sizes
    i = lax.axis_index("dp")
    z = lax.axis_index("expert")
    t = lax.axis_index("tensor")
    count, width = tokens.shape
    inner = gate.shape[1]
    total = experts * count
    rows = count // tensor
    cols = width // lanes
    half = cols // 2
    tile_f = min(TILE, inner)
    bufs = (x_buf, g_buf)

    def zz(k):
        return lax.rem(z + k, experts)

    def tt(s):
        return lax.rem(t + s, tensor)

    def row_ds(which):
        return pl.ds(pl.multiple_of(which * rows, rows), rows)

    def col_ds(which):
        return pl.ds(pl.multiple_of(which * cols, cols), cols)

    def half_ds(which, part):
        return pl.ds(pl.multiple_of(which * cols + part * half, half), half)

    def remote(src, dst, send, recv, axis, target):
        return pltpu.make_async_remote_copy(
            src_ref=src,
            dst_ref=dst,
            send_sem=send,
            recv_sem=recv,
            device_id={axis: target},
            device_id_type=MESH,
        )

    loads = {}

    def fetch(kind, m, slot, parts=(0, 1)):
        for part in parts:
            source = half_ds(flip(i, m), part)
            to = pl.ds(part * half, half)
            if kind == 0:
                pair = (w_gate.at[source, :], wg_buf.at[slot, to, :])
            elif kind == 1:
                pair = (w_up.at[source, :], wu_buf.at[slot, to, :])
            else:
                pair = (w_down.at[:, source], wd_buf.at[slot, :, to])
            copy = pltpu.make_async_copy(*pair, w_sem.at[kind, slot, part])
            copy.start()
            loads[kind, slot, part] = copy

    def fetched(kind, slot, parts=(0, 1)):
        for part in parts:
            copy = loads.pop((kind, slot, part), None)
            if copy is not None:
                copy.wait()

    own = [
        pltpu.make_async_copy(tokens, x_buf.at[z], own_sem.at[0]),
        pltpu.make_async_copy(grads, g_buf.at[z], own_sem.at[1]),
        pltpu.make_async_copy(table.at[z], share_rows.at[z], own_sem.at[2]),
    ]

    barrier = pltpu.get_barrier_semaphore()
    for k in range(1, experts):
        pl.semaphore_signal(barrier, inc=1, device_id={"expert": zz(k)}, device_id_type=MESH)
    for m in range(1, lanes):
        pl.semaphore_signal(barrier, inc=1, device_id={"dp": flip(i, m)}, device_id_type=MESH)
    for s in range(1, tensor):
        pl.semaphore_signal(barrier, inc=1, device_id={"tensor": tt(s)}, device_id_type=MESH)
    pl.semaphore_wait(barrier, experts + lanes + tensor - 3)

    def step_one(a):
        copies = []
        source = (tokens, grads)[a]
        for k in range(1, experts):
            copies.append(
                remote(
                    source.at[row_ds(t), col_ds(i)],
                    bufs[a].at[z, row_ds(t), col_ds(i)],
                    d1_send.at[a, k],
                    d1_recv.at[a, k],
                    "expert",
                    zz(k),
                )
            )
        for copy in copies:
            copy.start()
        return copies

    def step_two(a, k):
        place = bufs[a].at[zz(experts - k), row_ds(t), col_ds(i)]
        for m in (1, 2):
            copy = remote(
                place, place, d2_send.at[a, k, m], d2_recv.at[a, k, m], "dp", flip(i, m)
            )
            copy.start()
            second[a, k, m] = [copy]

    def step_across(a, k, m):
        place = bufs[a].at[zz(experts - k), row_ds(t), half_ds(flip(i, m), m - 1)]
        copy = remote(
            place, place, d2_send.at[a, k, m + 2], d2_recv.at[a, k, m + 2], "dp", flip(i, 3 - m)
        )
        copy.start()
        second.setdefault((a, k, 3), []).append(copy)

    def step_three(a, k, m):
        copies = []
        place = bufs[a].at[zz(experts - k), row_ds(t), col_ds(flip(i, m))]
        for s in range(1, tensor):
            copies.append(
                remote(
                    place, place, d3_send.at[a, k, m, s], d3_recv.at[a, k, m, s], "tensor", tt(s)
                )
            )
        for copy in copies:
            copy.start()
        return copies

    first = {0: step_one(0)}
    shares = []
    for k in range(1, experts):
        shares.append(
            remote(
                table.at[zz(k)],
                share_rows.at[z],
                t_send.at[k],
                t_recv.at[k],
                "expert",
                zz(k),
            )
        )
    for copy in shares:
        copy.start()
    for copy in own:
        copy.start()
    for slot in range(2):
        fetch(0, slot, slot)
        fetch(1, slot, slot)
    for slot in range(2):
        fetch(2, lanes - 1 - slot, slot)

    second = {}
    third = {}

    def relay_one(a, k):
        first[a][k - 1].wait_recv()
        step_two(a, k)
        third[a, k, 0] = step_three(a, k, 0)

    def relay_two(a, k, m):
        for copy in second[a, k, m]:
            copy.wait_recv()
        if m < 3:
            step_across(a, k, m)
        third[a, k, m] = step_three(a, k, m)

    def arrived(a, m):
        for k in range(1, experts):
            for copy in third[a, k, m]:
                copy.wait_recv()

    def sent(a):
        for copy in first[a]:
            copy.wait_send()
        for k in range(1, experts):
            for m in range(1, lanes):
                for copy in second[a, k, m]:
                    copy.wait_send()
            for m in range(lanes):
                for copy in third[a, k, m]:
                    copy.wait_send()

    def operand(a, m):
        return bufs[a][:, :, col_ds(flip(i, m))].reshape(total, cols)

    others = list(range(1, experts))
    for k in others:
        relay_one(0, k)
    first[1] = step_one(1)
    own[0].wait()
    for m in range(lanes):
        if m + 1 < lanes:
            for k in others:
                relay_two(0, k, m + 1)
        for k in others:
            if m == min(k, lanes - 1):
                relay_one(1, k)
        arrived(0, m)
        slot = m % 2
        fetched(0, slot)
        fetched(1, slot)

        def project(n, carry, m=m, slot=slot):
            span = pl.ds(pl.multiple_of(n * tile_f, tile_f), tile_f)
            left = operand(0, m)
            one = jnp.dot(left, wg_buf[slot, :, span], preferred_element_type=jnp.float32)
            two = jnp.dot(left, wu_buf[slot, :, span], preferred_element_type=jnp.float32)
            if m == 0:
                gate[:, span] = one
                up[:, span] = two
            else:
                gate[:, span] += one
                up[:, span] += two
            return carry

        lax.fori_loop(0, inner // tile_f, project, 0)
        if m + 2 < lanes:
            fetch(0, m + 2, slot)
            fetch(1, m + 2, slot)

    own[2].wait()
    for copy in shares:
        copy.wait()
    for e in range(experts):
        share_cols[e * count : (e + 1) * count, :] = jnp.broadcast_to(
            share_rows[e, 0:1, :], (count, count)
        ).T

    def activate(e, carry):
        span = pl.ds(pl.multiple_of(e * count, count), count)
        weight = share_cols[span, 0:1]
        for f in range(0, inner, tile_f):
            v = gate[span, f : f + tile_f]
            sig = jax.nn.sigmoid(v)
            hid[span, f : f + tile_f] = (v * sig * up[span, f : f + tile_f] * weight).astype(
                jnp.bfloat16
            )
        return carry

    lax.fori_loop(0, experts, activate, 0)
    sent(0)

    pairs = {}
    planes = {}
    vias = {}
    order = others + [0]

    def group_size(a):
        return cols // GROUPS[a]

    def group_ds(a, g, m):
        size = group_size(a)
        return pl.ds(pl.multiple_of(flip(i, m) * cols + g * size, size), size)

    def part_ds(a, g, m, part):
        size = group_size(a) // 2
        start = flip(i, m) * cols + (2 * g + part) * size
        return pl.ds(pl.multiple_of(start, size), size)

    def inside(a, g, part=None):
        size = group_size(a)
        if part is None:
            return pl.ds(g * size, size)
        return pl.ds((2 * g + part) * (size // 2), size // 2)

    def pair_send(a, g, m):
        copies = []
        for s in range(1, tensor):
            copies.append(
                remote(
                    bufs[a].at[:, row_ds(tt(s)), group_ds(a, g, m)],
                    pair_buf.at[a, m, s - 1, :, :, inside(a, g)],
                    r1_send.at[a, g, m, s],
                    r1_recv.at[a, g, m, s],
                    "tensor",
                    tt(s),
                )
            )
        for copy in copies:
            copy.start()
        pairs[a, g, m] = copies

    def pair_sum(a, g, m):
        for copy in pairs[a, g, m]:
            copy.wait_recv()
        block = group_ds(a, g, m)

        def add(e, carry):
            value = bufs[a][e, row_ds(t), block].astype(jnp.float32)
            for s in range(tensor - 1):
                value = value + pair_buf[a, m, s, e, :, inside(a, g)].astype(jnp.float32)
            bufs[a][e, row_ds(t), block] = value.astype(jnp.bfloat16)
            return carry

        lax.fori_loop(0, experts, add, 0)
        for k in order:
            if m == 3:
                for part in range(2):
                    copy = remote(
                        bufs[a].at[zz(k), row_ds(t), part_ds(a, g, 3, part)],
                        via_buf.at[a, part, zz(k), :, inside_via(a, g)],
                        via_send.at[a, g, part, k],
                        via_recv.at[a, g, part, k],
                        "dp",
                        flip(i, part + 1),
                    )
                    copy.start()
                    vias[a, g, part, k] = copy
            elif m > 0:
                plane_send(a, g, m, k, m - 1)

    def inside_via(a, g):
        size = group_size(a) // 2
        return pl.ds(g * size, size)

    def plane_send(a, g, m, k, part):
        copy = remote(
            bufs[a].at[zz(k), row_ds(t), part_ds(a, g, m, part)],
            plane_buf.at[a, m - 1, zz(k), :, inside(a, g, part)],
            r2_send.at[a, g, m - 1, part, k],
            r2_recv.at[a, g, m - 1, part, k],
            "dp",
            flip(i, m),
        )
        copy.start()
        planes[a, g, m, part, k] = copy

    def via_sum(a, g):
        for k in order:
            for part in range(2):
                m = 2 - part
                vias[a, g, part, k].wait_recv()
                place = bufs[a].at[zz(k), row_ds(t), part_ds(a, g, m, part)]
                value = place[...].astype(jnp.float32)
                value = value + via_buf[a, part, zz(k), :, inside_via(a, g)].astype(jnp.float32)
                place[...] = value.astype(jnp.bfloat16)
                plane_send(a, g, m, k, part)

    crossing = {}
    finals = []

    def plane_sum(a, g):
        for k in order:
            for m in (1, 2):
                for part in range(2):
                    planes[a, g, m, part, k].wait_recv()
            place = bufs[a].at[zz(k), row_ds(t), group_ds(a, g, 0)]
            value = place[...].astype(jnp.float32)
            for m in (1, 2):
                value = value + plane_buf[a, m - 1, zz(k), :, inside(a, g)].astype(jnp.float32)
            place[...] = value.astype(jnp.bfloat16)
            if k > 0:
                copy = remote(
                    place,
                    axis_buf.at[a, k - 1, :, inside(a, g)],
                    r3_send.at[a, g, k],
                    r3_recv.at[a, g, k],
                    "expert",
                    zz(k),
                )
                copy.start()
                crossing[a, g, k] = copy

    def finish(a, g):
        value = bufs[a][z, row_ds(t), group_ds(a, g, 0)].astype(jnp.float32)
        for k in others:
            crossing[a, g, k].wait_recv()
            value = value + axis_buf[a, k - 1, :, inside(a, g)].astype(jnp.float32)
        source = final_buf.at[a, :, inside(a, g)]
        source[...] = value.astype(jnp.bfloat16)
        target = (out_hbm, back_hbm)[a].at[:, group_ds(a, g, 0)]
        copies = []
        for m in range(lanes - 1, 0, -1):
            copies.append(
                remote(
                    source, target, r4_send.at[a, g, m], r4_recv.at[a, g, m], "dp", flip(i, m)
                )
            )
        copies.append(pltpu.make_async_copy(source, target, own_sem.at[3 + 2 * a + g]))
        for copy in copies:
            copy.start()
        finals.extend(copies)

    for n in range(lanes):
        m = lanes - 1 - n
        slot = n % 2
        fetched(2, slot)

        def down(c, carry, m=m, slot=slot):
            span = pl.ds(pl.multiple_of(c * half, half), half)
            to = half_ds(flip(i, m), c)
            value = jnp.dot(hid[...], wd_buf[slot, :, span], preferred_element_type=jnp.float32)
            x_buf[:, :, to] = value.astype(jnp.bfloat16).reshape(experts, count, half)
            return carry

        lax.fori_loop(0, 2, down, 0)
        if n + 2 < lanes:
            fetch(2, lanes - 1 - (n + 2), slot)
        pair_send(0, 0, m)
        if n > 0:
            pair_sum(0, 0, m + 1)
            for k in others:
                if n == min(k, lanes - 1):
                    relay_two(1, k, 1)
                    relay_two(1, k, 2)
    pair_sum(0, 0, 0)

    own[1].wait()
    for m in range(lanes):
        if m == lanes - 2:
            for k in others:
                relay_two(1, k, 3)
        arrived(1, m)
        slot = (lanes - 1 - m) % 2
        fetched(2, slot)

        def project_back(n, carry, m=m, slot=slot):
            span = pl.ds(pl.multiple_of(n * tile_f, tile_f), tile_f)
            value = lax.dot_general(
                operand(1, m),
                wd_buf[slot, span, :],
                CONTRACT_LAST,
                preferred_element_type=jnp.float32,
            )
            if m == 0:
                gh[:, span] = value
            else:
                gh[:, span] += value
            return carry

        lax.fori_loop(0, inner // tile_f, project_back, 0)
        if m + 2 < lanes:
            fetch(2, m + 2, slot)

    def differentiate(e, carry):
        span = pl.ds(pl.multiple_of(e * count, count), count)
        weight = share_cols[span, 0:1]
        for f in range(0, inner, tile_f):
            part = slice(f, f + tile_f)
            v = gate[span, part]
            sig = jax.nn.sigmoid(v)
            slope = gh[span, part] * weight * sig
            hid[span, part] = (slope * up[span, part] * (1.0 + v * (1.0 - sig))).astype(
                jnp.bfloat16
            )
            gu[span, part] = (slope * v).astype(jnp.bfloat16)
        return carry

    lax.fori_loop(0, experts, differentiate, 0)
    sent(1)

    steps = [(g, m) for g in range(2) for m in range(lanes - 1, -1, -1)]
    for step, (g, m) in enumerate(steps):
        slot = m % 2
        fetched(0, slot, (g,))
        fetched(1, slot, (g,))
        span = slice(g * half, (g + 1) * half)
        value = lax.dot_general(
            hid[...], wg_buf[slot, span, :], CONTRACT_LAST, preferred_element_type=jnp.float32
        )
        value = value + lax.dot_general(
            gu[...], wu_buf[slot, span, :], CONTRACT_LAST, preferred_element_type=jnp.float32
        )
        g_buf[:, :, half_ds(flip(i, m), g)] = value.astype(jnp.bfloat16).reshape(
            experts, count, half
        )
        if m >= 2:
            fetch(0, m - 2, slot, (g,))
            fetch(1, m - 2, slot, (g,))
        pair_send(1, g, m)
        if step > 0:
            pair_sum(1, *steps[step - 1])
        if step == 0:
            via_sum(0, 0)
        if step == 4:
            plane_sum(0, 0)
        if step == 5:
            via_sum(1, 0)
    pair_sum(1, 1, 0)
    finish(0, 0)
    plane_sum(1, 0)
    via_sum(1, 1)
    finish(1, 0)
    plane_sum(1, 1)
    finish(1, 1)
    for copies in pairs.values():
        for copy in copies:
            copy.wait_send()
    for copy in vias.values():
        copy.wait_send()
    for copy in planes.values():
        copy.wait_send()
    for copy in crossing.values():
        copy.wait_send()
    for copy in finals:
        copy.wait()


def local(sizes, tokens, routes, logits, grad_out, w_gate, w_up, w_down):
    lanes, experts, tensor = sizes
    count, width = tokens.shape
    inner = w_gate.shape[2]
    rows = count // tensor
    cols = width // lanes
    total = experts * count
    share = jax.nn.sigmoid(logits[:, 0] - logits[:, 1])
    labels = jnp.arange(experts, dtype=jnp.int32)[:, None]
    table = jnp.where(routes[None, :, 0] == labels, share[None, :], 0.0)
    table = table + jnp.where(routes[None, :, 1] == labels, 1.0 - share[None, :], 0.0)
    table = jnp.broadcast_to(table[:, None, :], (experts, 8, count))
    bf16 = jnp.bfloat16
    f32 = jnp.float32
    dma = pltpu.SemaphoreType.DMA
    result = jax.ShapeDtypeStruct((rows, width), bf16)
    anywhere = pl.BlockSpec(memory_space=pl.ANY)
    flops = 2 * total * width * inner * 6
    return pl.pallas_call(
        functools.partial(expert_kernel, sizes),
        out_shape=(result, result),
        in_specs=[anywhere] * 6,
        out_specs=(anywhere, anywhere),
        scratch_shapes=[
            pltpu.VMEM((experts, count, width), bf16),
            pltpu.VMEM((experts, count, width), bf16),
            pltpu.VMEM((2, cols, inner), bf16),
            pltpu.VMEM((2, cols, inner), bf16),
            pltpu.VMEM((2, inner, cols), bf16),
            pltpu.VMEM((total, inner), f32),
            pltpu.VMEM((total, inner), f32),
            pltpu.VMEM((total, inner), f32),
            pltpu.VMEM((total, inner), bf16),
            pltpu.VMEM((total, inner), bf16),
            pltpu.VMEM((experts, 8, count), f32),
            pltpu.VMEM((total, count), f32),
            pltpu.VMEM((2, lanes, tensor - 1, experts, rows, cols), bf16),
            pltpu.VMEM((2, 2, experts, rows, cols), bf16),
            pltpu.VMEM((2, 2, experts, rows, cols // 2), bf16),
            pltpu.VMEM((2, experts - 1, rows, cols), bf16),
            pltpu.VMEM((2, rows, cols), bf16),
            dma((3, 2, 2)),
            dma((7,)),
            dma((experts,)),
            dma((experts,)),
            dma((2, experts)),
            dma((2, experts)),
            dma((2, experts, 5)),
            dma((2, experts, 5)),
            dma((2, experts, lanes, tensor)),
            dma((2, experts, lanes, tensor)),
            dma((2, 2, lanes, tensor)),
            dma((2, 2, lanes, tensor)),
            dma((2, 2, 2, 2, experts)),
            dma((2, 2, 2, 2, experts)),
            dma((2, 2, 2, experts)),
            dma((2, 2, 2, experts)),
            dma((2, 2, experts)),
            dma((2, 2, experts)),
            dma((2, 2, lanes)),
            dma((2, 2, lanes)),
        ],
        compiler_params=pltpu.CompilerParams(
            collective_id=0, has_side_effects=True, vmem_limit_bytes=62 * 1024 * 1024
        ),
        cost_estimate=pl.CostEstimate(
            flops=flops, bytes_accessed=6 * width * inner * 2, transcendentals=2 * total * inner
        ),
        name="expert_layer",
    )(tokens, grad_out, table, w_gate[0], w_up[0], w_down[0])


def solution(mesh):
    sizes = (mesh.shape["dp"], mesh.shape["expert"], mesh.shape["tensor"])
    return jax.shard_map(
        functools.partial(local, sizes),
        mesh=mesh,
        in_specs=(
            P("expert", None),
            P("expert", None),
            P("expert", None),
            P("expert", None),
            P("expert", None, ("dp", "tensor")),
            P("expert", None, ("dp", "tensor")),
            P("expert", ("dp", "tensor"), None),
        ),
        out_specs=(P(("expert", "tensor"), None), P(("expert", "tensor"), None)),
        check_vma=False,
    )
```

```python
import functools

import jax
import jax.numpy as jnp
from jax import lax
from jax.experimental import pallas as pl
from jax.experimental.pallas import tpu as pltpu
from jax.sharding import PartitionSpec as P

MESH = pl.DeviceIdType.MESH
CONTRACT_LAST = (((1,), (1,)), ((), ()))
TILE = 512
GROUPS = (1, 2)


def flip(index, mask):
    out = index
    bit = 1
    while bit <= mask:
        if mask & bit:
            out = out + bit - 2 * bit * lax.rem(index // bit, 2)
        bit *= 2
    return out


def expert_kernel(
    sizes,
    tokens,
    grads,
    table,
    w_gate,
    w_up,
    w_down,
    out_hbm,
    back_hbm,
    x_buf,
    g_buf,
    wg_buf,
    wu_buf,
    wd_buf,
    gate,
    up,
    gh,
    hid,
    gu,
    share_rows,
    share_cols,
    pair_buf,
    plane_buf,
    via_buf,
    axis_buf,
    final_buf,
    w_sem,
    own_sem,
    t_send,
    t_recv,
    d1_send,
    d1_recv,
    d2_send,
    d2_recv,
    d3_send,
    d3_recv,
    r1_send,
    r1_recv,
    r2_send,
    r2_recv,
    via_send,
    via_recv,
    r3_send,
    r3_recv,
    r4_send,
    r4_recv,
):
    lanes, experts, tensor = sizes
    i = lax.axis_index("dp")
    z = lax.axis_index("expert")
    t = lax.axis_index("tensor")
    count, width = tokens.shape
    inner = gate.shape[1]
    total = experts * count
    rows = count // tensor
    cols = width // lanes
    half = cols // 2
    tile_f = min(TILE, inner)
    bufs = (x_buf, g_buf)

    def zz(k):
        return lax.rem(z + k, experts)

    def tt(s):
        return lax.rem(t + s, tensor)

    def row_ds(which):
        return pl.ds(pl.multiple_of(which * rows, rows), rows)

    def col_ds(which):
        return pl.ds(pl.multiple_of(which * cols, cols), cols)

    def half_ds(which, part):
        return pl.ds(pl.multiple_of(which * cols + part * half, half), half)

    def remote(src, dst, send, recv, axis, target):
        return pltpu.make_async_remote_copy(
            src_ref=src,
            dst_ref=dst,
            send_sem=send,
            recv_sem=recv,
            device_id={axis: target},
            device_id_type=MESH,
        )

    loads = {}

    def fetch(kind, m, slot, parts=(0, 1)):
        for part in parts:
            source = half_ds(flip(i, m), part)
            to = pl.ds(part * half, half)
            if kind == 0:
                pair = (w_gate.at[source, :], wg_buf.at[slot, to, :])
            elif kind == 1:
                pair = (w_up.at[source, :], wu_buf.at[slot, to, :])
            else:
                pair = (w_down.at[:, source], wd_buf.at[slot, :, to])
            copy = pltpu.make_async_copy(*pair, w_sem.at[kind, slot, part])
            copy.start()
            loads[kind, slot, part] = copy

    def fetched(kind, slot, parts=(0, 1)):
        for part in parts:
            copy = loads.pop((kind, slot, part), None)
            if copy is not None:
                copy.wait()

    own = [
        pltpu.make_async_copy(tokens, x_buf.at[z], own_sem.at[0]),
        pltpu.make_async_copy(grads, g_buf.at[z], own_sem.at[1]),
        pltpu.make_async_copy(table.at[z], share_rows.at[z], own_sem.at[2]),
    ]

    barrier = pltpu.get_barrier_semaphore()
    for k in range(1, experts):
        pl.semaphore_signal(barrier, inc=1, device_id={"expert": zz(k)}, device_id_type=MESH)
    for m in range(1, lanes):
        pl.semaphore_signal(barrier, inc=1, device_id={"dp": flip(i, m)}, device_id_type=MESH)
    for s in range(1, tensor):
        pl.semaphore_signal(barrier, inc=1, device_id={"tensor": tt(s)}, device_id_type=MESH)
    pl.semaphore_wait(barrier, experts + lanes + tensor - 3)

    others = sorted(range(1, experts), key=lambda k: min(k, experts - k))
    first = {}

    def step_one(a, k):
        copy = remote(
            (tokens, grads)[a].at[row_ds(t), col_ds(i)],
            bufs[a].at[z, row_ds(t), col_ds(i)],
            d1_send.at[a, k],
            d1_recv.at[a, k],
            "expert",
            zz(k),
        )
        copy.start()
        first[a, k] = copy

    def step_two(a, k):
        place = bufs[a].at[zz(experts - k), row_ds(t), col_ds(i)]
        for m in (1, 2):
            copy = remote(
                place, place, d2_send.at[a, k, m], d2_recv.at[a, k, m], "dp", flip(i, m)
            )
            copy.start()
            second[a, k, m] = [copy]

    def step_across(a, k, m):
        place = bufs[a].at[zz(experts - k), row_ds(t), half_ds(flip(i, m), m - 1)]
        copy = remote(
            place, place, d2_send.at[a, k, m + 2], d2_recv.at[a, k, m + 2], "dp", flip(i, 3 - m)
        )
        copy.start()
        second.setdefault((a, k, 3), []).append(copy)

    def step_three(a, k, m):
        copies = []
        place = bufs[a].at[zz(experts - k), row_ds(t), col_ds(flip(i, m))]
        for s in range(1, tensor):
            copies.append(
                remote(
                    place, place, d3_send.at[a, k, m, s], d3_recv.at[a, k, m, s], "tensor", tt(s)
                )
            )
        for copy in copies:
            copy.start()
        return copies

    step_one(0, others[0])
    shares = []
    for k in range(1, experts):
        shares.append(
            remote(
                table.at[zz(k)],
                share_rows.at[z],
                t_send.at[k],
                t_recv.at[k],
                "expert",
                zz(k),
            )
        )
    for copy in shares:
        copy.start()
    for copy in own:
        copy.start()
    for slot in range(2):
        fetch(0, slot, slot)
        fetch(1, slot, slot)
    for slot in range(2):
        fetch(2, lanes - 1 - slot, slot)

    second = {}
    third = {}
    left = set()

    def relay_one(a, k):
        first[a, k].wait_recv()
        step_two(a, k)
        third[a, k, 0] = step_three(a, k, 0)

    def relay_two(a, k, m):
        for copy in second[a, k, m]:
            copy.wait_recv()
        if m < 3:
            step_across(a, k, m)
        third[a, k, m] = step_three(a, k, m)

    def arrived(a, m):
        for k in range(1, experts):
            for copy in third[a, k, m]:
                copy.wait_recv()

    def sent(a):
        for k in others:
            if (a, k) not in left:
                first[a, k].wait_send()
            for m in range(1, lanes):
                for copy in second[a, k, m]:
                    copy.wait_send()
            for m in range(lanes):
                for copy in third[a, k, m]:
                    copy.wait_send()

    def operand(a, m):
        return bufs[a][:, :, col_ds(flip(i, m))].reshape(total, cols)

    def follow(a, k, b, n):
        first[a, k].wait_send()
        left.add((a, k))
        step_one(b, n)

    for n, k in enumerate(others):
        if n + 1 < len(others):
            follow(0, k, 0, others[n + 1])
        else:
            follow(0, k, 1, others[0])
        relay_one(0, k)
        if n > 0:
            relay_two(0, others[n - 1], 1)
            relay_two(0, others[n - 1], 2)
    own[0].wait()
    for m in range(lanes):
        if m == 1:
            relay_two(0, others[-1], 1)
            relay_two(0, others[-1], 2)
        for n, k in enumerate(others):
            if m == min(n + 1, lanes - 1):
                if n + 1 < len(others):
                    follow(1, k, 1, others[n + 1])
                relay_one(1, k)
        if m == lanes - 1:
            for k in others:
                relay_two(0, k, 3)
        arrived(0, m)
        slot = m % 2
        fetched(0, slot)
        fetched(1, slot)

        def project(n, carry, m=m, slot=slot):
            span = pl.ds(pl.multiple_of(n * tile_f, tile_f), tile_f)
            left = operand(0, m)
            one = jnp.dot(left, wg_buf[slot, :, span], preferred_element_type=jnp.float32)
            two = jnp.dot(left, wu_buf[slot, :, span], preferred_element_type=jnp.float32)
            if m == 0:
                gate[:, span] = one
                up[:, span] = two
            else:
                gate[:, span] += one
                up[:, span] += two
            return carry

        lax.fori_loop(0, inner // tile_f, project, 0)
        if m + 2 < lanes:
            fetch(0, m + 2, slot)
            fetch(1, m + 2, slot)

    own[2].wait()
    for copy in shares:
        copy.wait()
    for e in range(experts):
        share_cols[e * count : (e + 1) * count, :] = jnp.broadcast_to(
            share_rows[e, 0:1, :], (count, count)
        ).T

    def activate(e, carry):
        span = pl.ds(pl.multiple_of(e * count, count), count)
        weight = share_cols[span, 0:1]
        for f in range(0, inner, tile_f):
            v = gate[span, f : f + tile_f]
            sig = jax.nn.sigmoid(v)
            hid[span, f : f + tile_f] = (v * sig * up[span, f : f + tile_f] * weight).astype(
                jnp.bfloat16
            )
        return carry

    lax.fori_loop(0, experts, activate, 0)
    sent(0)

    pairs = {}
    planes = {}
    vias = {}
    order = others[::-1] + [0]

    def group_size(a):
        return cols // GROUPS[a]

    def group_ds(a, g, m):
        size = group_size(a)
        return pl.ds(pl.multiple_of(flip(i, m) * cols + g * size, size), size)

    def part_ds(a, g, m, part):
        size = group_size(a) // 2
        start = flip(i, m) * cols + (2 * g + part) * size
        return pl.ds(pl.multiple_of(start, size), size)

    def inside(a, g, part=None):
        size = group_size(a)
        if part is None:
            return pl.ds(g * size, size)
        return pl.ds((2 * g + part) * (size // 2), size // 2)

    def pair_send(a, g, m):
        copies = []
        for s in range(1, tensor):
            copies.append(
                remote(
                    bufs[a].at[:, row_ds(tt(s)), group_ds(a, g, m)],
                    pair_buf.at[a, m, s - 1, :, :, inside(a, g)],
                    r1_send.at[a, g, m, s],
                    r1_recv.at[a, g, m, s],
                    "tensor",
                    tt(s),
                )
            )
        for copy in copies:
            copy.start()
        pairs[a, g, m] = copies

    def pair_sum(a, g, m):
        for copy in pairs[a, g, m]:
            copy.wait_recv()
        block = group_ds(a, g, m)

        def add(e, carry):
            value = bufs[a][e, row_ds(t), block].astype(jnp.float32)
            for s in range(tensor - 1):
                value = value + pair_buf[a, m, s, e, :, inside(a, g)].astype(jnp.float32)
            bufs[a][e, row_ds(t), block] = value.astype(jnp.bfloat16)
            return carry

        lax.fori_loop(0, experts, add, 0)
        for k in order:
            if m == 3:
                for part in range(2):
                    copy = remote(
                        bufs[a].at[zz(k), row_ds(t), part_ds(a, g, 3, part)],
                        via_buf.at[a, part, zz(k), :, inside_via(a, g)],
                        via_send.at[a, g, part, k],
                        via_recv.at[a, g, part, k],
                        "dp",
                        flip(i, part + 1),
                    )
                    copy.start()
                    vias[a, g, part, k] = copy
            elif m > 0:
                plane_send(a, g, m, k, m - 1)

    def inside_via(a, g):
        size = group_size(a) // 2
        return pl.ds(g * size, size)

    def plane_send(a, g, m, k, part):
        copy = remote(
            bufs[a].at[zz(k), row_ds(t), part_ds(a, g, m, part)],
            plane_buf.at[a, m - 1, zz(k), :, inside(a, g, part)],
            r2_send.at[a, g, m - 1, part, k],
            r2_recv.at[a, g, m - 1, part, k],
            "dp",
            flip(i, m),
        )
        copy.start()
        planes[a, g, m, part, k] = copy

    def via_sum(a, g):
        for k in order:
            for part in range(2):
                m = 2 - part
                vias[a, g, part, k].wait_recv()
                place = bufs[a].at[zz(k), row_ds(t), part_ds(a, g, m, part)]
                value = place[...].astype(jnp.float32)
                value = value + via_buf[a, part, zz(k), :, inside_via(a, g)].astype(jnp.float32)
                place[...] = value.astype(jnp.bfloat16)
                plane_send(a, g, m, k, part)

    crossing = {}
    finals = []

    def plane_sum(a, g):
        for k in order:
            for m in (1, 2):
                for part in range(2):
                    planes[a, g, m, part, k].wait_recv()
            place = bufs[a].at[zz(k), row_ds(t), group_ds(a, g, 0)]
            value = place[...].astype(jnp.float32)
            for m in (1, 2):
                value = value + plane_buf[a, m - 1, zz(k), :, inside(a, g)].astype(jnp.float32)
            place[...] = value.astype(jnp.bfloat16)
            if k > 0:
                copy = remote(
                    place,
                    axis_buf.at[a, k - 1, :, inside(a, g)],
                    r3_send.at[a, g, k],
                    r3_recv.at[a, g, k],
                    "expert",
                    zz(k),
                )
                copy.start()
                crossing[a, g, k] = copy

    def finish(a, g):
        value = bufs[a][z, row_ds(t), group_ds(a, g, 0)].astype(jnp.float32)
        for k in others:
            crossing[a, g, k].wait_recv()
            value = value + axis_buf[a, k - 1, :, inside(a, g)].astype(jnp.float32)
        source = final_buf.at[a, :, inside(a, g)]
        source[...] = value.astype(jnp.bfloat16)
        target = (out_hbm, back_hbm)[a].at[:, group_ds(a, g, 0)]
        copies = []
        for m in range(lanes - 1, 0, -1):
            copies.append(
                remote(
                    source, target, r4_send.at[a, g, m], r4_recv.at[a, g, m], "dp", flip(i, m)
                )
            )
        copies.append(pltpu.make_async_copy(source, target, own_sem.at[3 + 2 * a + g]))
        for copy in copies:
            copy.start()
        finals.extend(copies)

    for n in range(lanes):
        m = lanes - 1 - n
        slot = n % 2
        fetched(2, slot)

        def down(c, carry, m=m, slot=slot):
            span = pl.ds(pl.multiple_of(c * half, half), half)
            to = half_ds(flip(i, m), c)
            value = jnp.dot(hid[...], wd_buf[slot, :, span], preferred_element_type=jnp.float32)
            x_buf[:, :, to] = value.astype(jnp.bfloat16).reshape(experts, count, half)
            return carry

        lax.fori_loop(0, 2, down, 0)
        if n + 2 < lanes:
            fetch(2, lanes - 1 - (n + 2), slot)
        pair_send(0, 0, m)
        if n > 0:
            pair_sum(0, 0, m + 1)
            for j, k in enumerate(others):
                if n == min(j + 1, lanes - 1):
                    relay_two(1, k, 1)
                    relay_two(1, k, 2)
    pair_sum(0, 0, 0)

    own[1].wait()
    for m in range(lanes):
        if m == lanes - 2:
            for k in others:
                relay_two(1, k, 3)
        arrived(1, m)
        slot = (lanes - 1 - m) % 2
        fetched(2, slot)

        def project_back(n, carry, m=m, slot=slot):
            span = pl.ds(pl.multiple_of(n * tile_f, tile_f), tile_f)
            value = lax.dot_general(
                operand(1, m),
                wd_buf[slot, span, :],
                CONTRACT_LAST,
                preferred_element_type=jnp.float32,
            )
            if m == 0:
                gh[:, span] = value
            else:
                gh[:, span] += value
            return carry

        lax.fori_loop(0, inner // tile_f, project_back, 0)
        if m + 2 < lanes:
            fetch(2, m + 2, slot)

    def differentiate(e, carry):
        span = pl.ds(pl.multiple_of(e * count, count), count)
        weight = share_cols[span, 0:1]
        for f in range(0, inner, tile_f):
            part = slice(f, f + tile_f)
            v = gate[span, part]
            sig = jax.nn.sigmoid(v)
            slope = gh[span, part] * weight * sig
            hid[span, part] = (slope * up[span, part] * (1.0 + v * (1.0 - sig))).astype(
                jnp.bfloat16
            )
            gu[span, part] = (slope * v).astype(jnp.bfloat16)
        return carry

    lax.fori_loop(0, experts, differentiate, 0)
    sent(1)

    steps = [(g, m) for g in range(2) for m in range(lanes - 1, -1, -1)]
    for step, (g, m) in enumerate(steps):
        slot = m % 2
        fetched(0, slot, (g,))
        fetched(1, slot, (g,))
        span = slice(g * half, (g + 1) * half)
        value = lax.dot_general(
            hid[...], wg_buf[slot, span, :], CONTRACT_LAST, preferred_element_type=jnp.float32
        )
        value = value + lax.dot_general(
            gu[...], wu_buf[slot, span, :], CONTRACT_LAST, preferred_element_type=jnp.float32
        )
        g_buf[:, :, half_ds(flip(i, m), g)] = value.astype(jnp.bfloat16).reshape(
            experts, count, half
        )
        if m >= 2:
            fetch(0, m - 2, slot, (g,))
            fetch(1, m - 2, slot, (g,))
        pair_send(1, g, m)
        if step > 0:
            pair_sum(1, *steps[step - 1])
        if step == 0:
            via_sum(0, 0)
        if step == 4:
            plane_sum(0, 0)
        if step == 5:
            via_sum(1, 0)
    pair_sum(1, 1, 0)
    finish(0, 0)
    plane_sum(1, 0)
    via_sum(1, 1)
    finish(1, 0)
    plane_sum(1, 1)
    finish(1, 1)
    for copies in pairs.values():
        for copy in copies:
            copy.wait_send()
    for copy in vias.values():
        copy.wait_send()
    for copy in planes.values():
        copy.wait_send()
    for copy in crossing.values():
        copy.wait_send()
    for copy in finals:
        copy.wait()


def hand_over(out, back, out_copy, back_copy, sem):
    rows = out.shape[0]
    parts = 4 if rows % 64 == 0 else 1
    span = rows // parts
    copies = []
    for a, (source, target) in enumerate(((out, out_copy), (back, back_copy))):
        for n in range(parts):
            part = pl.ds(n * span, span)
            copies.append(pltpu.make_async_copy(source.at[part], target.at[part], sem.at[a, n]))
    for copy in copies:
        copy.start()
    for copy in copies:
        copy.wait()


def local(sizes, tokens, routes, logits, grad_out, w_gate, w_up, w_down):
    lanes, experts, tensor = sizes
    count, width = tokens.shape
    inner = w_gate.shape[2]
    rows = count // tensor
    cols = width // lanes
    total = experts * count
    share = jax.nn.sigmoid(logits[:, 0] - logits[:, 1])
    labels = jnp.arange(experts, dtype=jnp.int32)[:, None]
    table = jnp.where(routes[None, :, 0] == labels, share[None, :], 0.0)
    table = table + jnp.where(routes[None, :, 1] == labels, 1.0 - share[None, :], 0.0)
    table = jnp.broadcast_to(table[:, None, :], (experts, 8, count))
    bf16 = jnp.bfloat16
    f32 = jnp.float32
    dma = pltpu.SemaphoreType.DMA
    result = jax.ShapeDtypeStruct((rows, width), bf16)
    anywhere = pl.BlockSpec(memory_space=pl.ANY)
    flops = 2 * total * width * inner * 6
    results = pl.pallas_call(
        functools.partial(expert_kernel, sizes),
        out_shape=(result, result),
        in_specs=[anywhere] * 6,
        out_specs=(anywhere, anywhere),
        scratch_shapes=[
            pltpu.VMEM((experts, count, width), bf16),
            pltpu.VMEM((experts, count, width), bf16),
            pltpu.VMEM((2, cols, inner), bf16),
            pltpu.VMEM((2, cols, inner), bf16),
            pltpu.VMEM((2, inner, cols), bf16),
            pltpu.VMEM((total, inner), f32),
            pltpu.VMEM((total, inner), f32),
            pltpu.VMEM((total, inner), f32),
            pltpu.VMEM((total, inner), bf16),
            pltpu.VMEM((total, inner), bf16),
            pltpu.VMEM((experts, 8, count), f32),
            pltpu.VMEM((total, count), f32),
            pltpu.VMEM((2, lanes, tensor - 1, experts, rows, cols), bf16),
            pltpu.VMEM((2, 2, experts, rows, cols), bf16),
            pltpu.VMEM((2, 2, experts, rows, cols // 2), bf16),
            pltpu.VMEM((2, experts - 1, rows, cols), bf16),
            pltpu.VMEM((2, rows, cols), bf16),
            dma((3, 2, 2)),
            dma((7,)),
            dma((experts,)),
            dma((experts,)),
            dma((2, experts)),
            dma((2, experts)),
            dma((2, experts, 5)),
            dma((2, experts, 5)),
            dma((2, experts, lanes, tensor)),
            dma((2, experts, lanes, tensor)),
            dma((2, 2, lanes, tensor)),
            dma((2, 2, lanes, tensor)),
            dma((2, 2, 2, 2, experts)),
            dma((2, 2, 2, 2, experts)),
            dma((2, 2, 2, experts)),
            dma((2, 2, 2, experts)),
            dma((2, 2, experts)),
            dma((2, 2, experts)),
            dma((2, 2, lanes)),
            dma((2, 2, lanes)),
        ],
        compiler_params=pltpu.CompilerParams(
            collective_id=0, has_side_effects=True, vmem_limit_bytes=62 * 1024 * 1024
        ),
        cost_estimate=pl.CostEstimate(
            flops=flops, bytes_accessed=6 * width * inner * 2, transcendentals=2 * total * inner
        ),
        name="expert_layer",
    )(tokens, grad_out, table, w_gate[0], w_up[0], w_down[0])
    return pl.pallas_call(
        hand_over,
        out_shape=(result, result),
        in_specs=[anywhere] * 2,
        out_specs=(anywhere, anywhere),
        scratch_shapes=[dma((2, 4))],
        name="hand_over",
    )(*results)


def solution(mesh):
    sizes = (mesh.shape["dp"], mesh.shape["expert"], mesh.shape["tensor"])
    return jax.shard_map(
        functools.partial(local, sizes),
        mesh=mesh,
        in_specs=(
            P("expert", None),
            P("expert", None),
            P("expert", None),
            P("expert", None),
            P("expert", None, ("dp", "tensor")),
            P("expert", None, ("dp", "tensor")),
            P("expert", ("dp", "tensor"), None),
        ),
        out_specs=(P(("expert", "tensor"), None), P(("expert", "tensor"), None)),
        check_vma=False,
    )
```

```python
import functools

import jax
import jax.numpy as jnp
from jax import lax
from jax.experimental import pallas as pl
from jax.experimental.pallas import tpu as pltpu
from jax.sharding import PartitionSpec as P

MESH = pl.DeviceIdType.MESH
CONTRACT_LAST = (((1,), (1,)), ((), ()))
TILE = 512
GROUPS = (1, 3)


def flip(index, mask):
    out = index
    bit = 1
    while bit <= mask:
        if mask & bit:
            out = out + bit - 2 * bit * lax.rem(index // bit, 2)
        bit *= 2
    return out


def expert_kernel(
    sizes,
    tokens,
    grads,
    table,
    w_gate,
    w_up,
    w_down,
    out_hbm,
    back_hbm,
    x_buf,
    g_buf,
    wg_buf,
    wu_buf,
    wd_buf,
    gate,
    up,
    gh,
    hid,
    gu,
    share_rows,
    share_cols,
    pair_buf,
    plane_buf,
    via_buf,
    axis_buf,
    final_buf,
    w_sem,
    own_sem,
    t_send,
    t_recv,
    d1_send,
    d1_recv,
    d2_send,
    d2_recv,
    d3_send,
    d3_recv,
    r1_send,
    r1_recv,
    r2_send,
    r2_recv,
    via_send,
    via_recv,
    r3_send,
    r3_recv,
    r4_send,
    r4_recv,
):
    lanes, experts, tensor = sizes
    i = lax.axis_index("dp")
    z = lax.axis_index("expert")
    t = lax.axis_index("tensor")
    count, width = tokens.shape
    inner = gate.shape[1]
    total = experts * count
    rows = count // tensor
    cols = width // lanes
    half = cols // 2
    slim = cols // 3
    tile_f = min(TILE, inner)
    bufs = (x_buf, g_buf)

    def zz(k):
        return lax.rem(z + k, experts)

    def tt(s):
        return lax.rem(t + s, tensor)

    def row_ds(which):
        return pl.ds(pl.multiple_of(which * rows, rows), rows)

    def col_ds(which):
        return pl.ds(pl.multiple_of(which * cols, cols), cols)

    def half_ds(which, part):
        return pl.ds(pl.multiple_of(which * cols + part * half, half), half)

    def slim_ds(which, part):
        return pl.ds(pl.multiple_of(which * cols + part * slim, slim), slim)

    def remote(src, dst, send, recv, axis, target):
        return pltpu.make_async_remote_copy(
            src_ref=src,
            dst_ref=dst,
            send_sem=send,
            recv_sem=recv,
            device_id={axis: target},
            device_id_type=MESH,
        )

    loads = {}

    def fetch(kind, m, slot, parts=(0, 1, 2)):
        for part in parts:
            source = slim_ds(flip(i, m), part)
            to = pl.ds(part * slim, slim)
            if kind == 0:
                pair = (w_gate.at[source, :], wg_buf.at[slot, to, :])
            elif kind == 1:
                pair = (w_up.at[source, :], wu_buf.at[slot, to, :])
            else:
                pair = (w_down.at[:, source], wd_buf.at[slot, :, to])
            copy = pltpu.make_async_copy(*pair, w_sem.at[kind, slot, part])
            copy.start()
            loads[kind, slot, part] = copy

    def fetched(kind, slot, parts=(0, 1, 2)):
        for part in parts:
            copy = loads.pop((kind, slot, part), None)
            if copy is not None:
                copy.wait()

    own = [
        pltpu.make_async_copy(tokens, x_buf.at[z], own_sem.at[0]),
        pltpu.make_async_copy(grads, g_buf.at[z], own_sem.at[1]),
        pltpu.make_async_copy(table.at[z], share_rows.at[z], own_sem.at[2]),
    ]

    barrier = pltpu.get_barrier_semaphore()
    for k in range(1, experts):
        pl.semaphore_signal(barrier, inc=1, device_id={"expert": zz(k)}, device_id_type=MESH)
    for m in range(1, lanes):
        pl.semaphore_signal(barrier, inc=1, device_id={"dp": flip(i, m)}, device_id_type=MESH)
    for s in range(1, tensor):
        pl.semaphore_signal(barrier, inc=1, device_id={"tensor": tt(s)}, device_id_type=MESH)
    pl.semaphore_wait(barrier, experts + lanes + tensor - 3)

    def step_one(a):
        copies = []
        source = (tokens, grads)[a]
        for k in range(1, experts):
            copies.append(
                remote(
                    source.at[row_ds(t), col_ds(i)],
                    bufs[a].at[z, row_ds(t), col_ds(i)],
                    d1_send.at[a, k],
                    d1_recv.at[a, k],
                    "expert",
                    zz(k),
                )
            )
        for copy in copies:
            copy.start()
        return copies

    def step_two(a, k):
        place = bufs[a].at[zz(experts - k), row_ds(t), col_ds(i)]
        for m in (1, 2):
            copy = remote(
                place, place, d2_send.at[a, k, m], d2_recv.at[a, k, m], "dp", flip(i, m)
            )
            copy.start()
            second[a, k, m] = [copy]

    def step_across(a, k, m):
        place = bufs[a].at[zz(experts - k), row_ds(t), half_ds(flip(i, m), m - 1)]
        copy = remote(
            place, place, d2_send.at[a, k, m + 2], d2_recv.at[a, k, m + 2], "dp", flip(i, 3 - m)
        )
        copy.start()
        second.setdefault((a, k, 3), []).append(copy)

    def step_three(a, k, m):
        copies = []
        place = bufs[a].at[zz(experts - k), row_ds(t), col_ds(flip(i, m))]
        for s in range(1, tensor):
            copies.append(
                remote(
                    place, place, d3_send.at[a, k, m, s], d3_recv.at[a, k, m, s], "tensor", tt(s)
                )
            )
        for copy in copies:
            copy.start()
        return copies

    first = {0: step_one(0)}
    shares = []
    for k in range(1, experts):
        shares.append(
            remote(
                table.at[zz(k)],
                share_rows.at[z],
                t_send.at[k],
                t_recv.at[k],
                "expert",
                zz(k),
            )
        )
    for copy in shares:
        copy.start()
    for copy in own:
        copy.start()
    for slot in range(2):
        fetch(0, slot, slot)
        fetch(1, slot, slot)
    for slot in range(2):
        fetch(2, lanes - 1 - slot, slot)

    second = {}
    third = {}

    def relay_one(a, k):
        first[a][k - 1].wait_recv()
        step_two(a, k)
        third[a, k, 0] = step_three(a, k, 0)

    def relay_two(a, k, m):
        for copy in second[a, k, m]:
            copy.wait_recv()
        if m < 3:
            step_across(a, k, m)
        third[a, k, m] = step_three(a, k, m)

    def arrived(a, m):
        for k in range(1, experts):
            for copy in third[a, k, m]:
                copy.wait_recv()

    def sent(a):
        for copy in first[a]:
            copy.wait_send()
        for k in range(1, experts):
            for m in range(1, lanes):
                for copy in second[a, k, m]:
                    copy.wait_send()
            for m in range(lanes):
                for copy in third[a, k, m]:
                    copy.wait_send()

    def operand(a, m):
        return bufs[a][:, :, col_ds(flip(i, m))].reshape(total, cols)

    others = list(range(1, experts))
    for k in others:
        relay_one(0, k)
    first[1] = step_one(1)
    own[0].wait()
    for m in range(lanes):
        if m + 1 < lanes:
            for k in others:
                relay_two(0, k, m + 1)
        for k in others:
            if m == min(k, lanes - 1):
                relay_one(1, k)
        arrived(0, m)
        slot = m % 2
        fetched(0, slot)
        fetched(1, slot)

        def project(n, carry, m=m, slot=slot):
            span = pl.ds(pl.multiple_of(n * tile_f, tile_f), tile_f)
            left = operand(0, m)
            one = jnp.dot(left, wg_buf[slot, :, span], preferred_element_type=jnp.float32)
            two = jnp.dot(left, wu_buf[slot, :, span], preferred_element_type=jnp.float32)
            if m == 0:
                gate[:, span] = one
                up[:, span] = two
            else:
                gate[:, span] += one
                up[:, span] += two
            return carry

        lax.fori_loop(0, inner // tile_f, project, 0)
        if m + 2 < lanes:
            fetch(0, m + 2, slot)
            fetch(1, m + 2, slot)

    own[2].wait()
    for copy in shares:
        copy.wait()
    for e in range(experts):
        share_cols[e * count : (e + 1) * count, :] = jnp.broadcast_to(
            share_rows[e, 0:1, :], (count, count)
        ).T

    def activate(e, carry):
        span = pl.ds(pl.multiple_of(e * count, count), count)
        weight = share_cols[span, 0:1]
        for f in range(0, inner, tile_f):
            v = gate[span, f : f + tile_f]
            sig = jax.nn.sigmoid(v)
            hid[span, f : f + tile_f] = (v * sig * up[span, f : f + tile_f] * weight).astype(
                jnp.bfloat16
            )
        return carry

    lax.fori_loop(0, experts, activate, 0)
    sent(0)

    pairs = {}
    planes = {}
    vias = {}
    order = others + [0]

    def group_size(a):
        return cols // GROUPS[a]

    def group_ds(a, g, m):
        size = group_size(a)
        return pl.ds(pl.multiple_of(flip(i, m) * cols + g * size, size), size)

    def part_ds(a, g, m, part):
        size = group_size(a) // 2
        start = flip(i, m) * cols + (2 * g + part) * size
        return pl.ds(pl.multiple_of(start, size), size)

    def inside(a, g, part=None):
        size = group_size(a)
        if part is None:
            return pl.ds(g * size, size)
        return pl.ds((2 * g + part) * (size // 2), size // 2)

    def pair_send(a, g, m):
        copies = []
        for s in range(1, tensor):
            copies.append(
                remote(
                    bufs[a].at[:, row_ds(tt(s)), group_ds(a, g, m)],
                    pair_buf.at[a, m, s - 1, :, :, inside(a, g)],
                    r1_send.at[a, g, m, s],
                    r1_recv.at[a, g, m, s],
                    "tensor",
                    tt(s),
                )
            )
        for copy in copies:
            copy.start()
        pairs[a, g, m] = copies

    def pair_sum(a, g, m):
        for copy in pairs[a, g, m]:
            copy.wait_recv()
        block = group_ds(a, g, m)

        def add(e, carry):
            value = bufs[a][e, row_ds(t), block].astype(jnp.float32)
            for s in range(tensor - 1):
                value = value + pair_buf[a, m, s, e, :, inside(a, g)].astype(jnp.float32)
            bufs[a][e, row_ds(t), block] = value.astype(jnp.bfloat16)
            return carry

        lax.fori_loop(0, experts, add, 0)
        for k in order:
            if m == 3:
                for part in range(2):
                    copy = remote(
                        bufs[a].at[zz(k), row_ds(t), part_ds(a, g, 3, part)],
                        via_buf.at[a, part, zz(k), :, inside_via(a, g)],
                        via_send.at[a, g, part, k],
                        via_recv.at[a, g, part, k],
                        "dp",
                        flip(i, part + 1),
                    )
                    copy.start()
                    vias[a, g, part, k] = copy
            elif m > 0:
                plane_send(a, g, m, k, m - 1)

    def inside_via(a, g):
        size = group_size(a) // 2
        return pl.ds(g * size, size)

    def plane_send(a, g, m, k, part):
        copy = remote(
            bufs[a].at[zz(k), row_ds(t), part_ds(a, g, m, part)],
            plane_buf.at[a, m - 1, zz(k), :, inside(a, g, part)],
            r2_send.at[a, g, m - 1, part, k],
            r2_recv.at[a, g, m - 1, part, k],
            "dp",
            flip(i, m),
        )
        copy.start()
        planes[a, g, m, part, k] = copy

    def via_sum(a, g):
        for k in order:
            for part in range(2):
                m = 2 - part
                vias[a, g, part, k].wait_recv()
                place = bufs[a].at[zz(k), row_ds(t), part_ds(a, g, m, part)]
                value = place[...].astype(jnp.float32)
                value = value + via_buf[a, part, zz(k), :, inside_via(a, g)].astype(jnp.float32)
                place[...] = value.astype(jnp.bfloat16)
                plane_send(a, g, m, k, part)

    crossing = {}
    finals = []

    def plane_sum(a, g):
        for k in order:
            for m in (1, 2):
                for part in range(2):
                    planes[a, g, m, part, k].wait_recv()
            place = bufs[a].at[zz(k), row_ds(t), group_ds(a, g, 0)]
            value = place[...].astype(jnp.float32)
            for m in (1, 2):
                value = value + plane_buf[a, m - 1, zz(k), :, inside(a, g)].astype(jnp.float32)
            place[...] = value.astype(jnp.bfloat16)
            if k > 0:
                copy = remote(
                    place,
                    axis_buf.at[a, k - 1, :, inside(a, g)],
                    r3_send.at[a, g, k],
                    r3_recv.at[a, g, k],
                    "expert",
                    zz(k),
                )
                copy.start()
                crossing[a, g, k] = copy

    def finish(a, g):
        value = bufs[a][z, row_ds(t), group_ds(a, g, 0)].astype(jnp.float32)
        for k in others:
            crossing[a, g, k].wait_recv()
            value = value + axis_buf[a, k - 1, :, inside(a, g)].astype(jnp.float32)
        source = final_buf.at[a, :, inside(a, g)]
        source[...] = value.astype(jnp.bfloat16)
        target = (out_hbm, back_hbm)[a].at[:, group_ds(a, g, 0)]
        copies = []
        for m in range(lanes - 1, 0, -1):
            copies.append(
                remote(
                    source, target, r4_send.at[a, g, m], r4_recv.at[a, g, m], "dp", flip(i, m)
                )
            )
        copies.append(pltpu.make_async_copy(source, target, own_sem.at[3 + 3 * a + g]))
        for copy in copies:
            copy.start()
        finals.extend(copies)

    for n in range(lanes):
        m = lanes - 1 - n
        slot = n % 2
        fetched(2, slot)

        def down(c, carry, m=m, slot=slot):
            span = pl.ds(pl.multiple_of(c * half, half), half)
            to = half_ds(flip(i, m), c)
            value = jnp.dot(hid[...], wd_buf[slot, :, span], preferred_element_type=jnp.float32)
            x_buf[:, :, to] = value.astype(jnp.bfloat16).reshape(experts, count, half)
            return carry

        lax.fori_loop(0, 2, down, 0)
        if n + 2 < lanes:
            fetch(2, lanes - 1 - (n + 2), slot)
        pair_send(0, 0, m)
        if n > 0:
            pair_sum(0, 0, m + 1)
            for k in others:
                if n == min(k, lanes - 1):
                    relay_two(1, k, 1)
                    relay_two(1, k, 2)
    pair_sum(0, 0, 0)

    own[1].wait()
    for m in range(lanes):
        if m == lanes - 2:
            for k in others:
                relay_two(1, k, 3)
        arrived(1, m)
        slot = (lanes - 1 - m) % 2
        fetched(2, slot)

        def project_back(n, carry, m=m, slot=slot):
            span = pl.ds(pl.multiple_of(n * tile_f, tile_f), tile_f)
            value = lax.dot_general(
                operand(1, m),
                wd_buf[slot, span, :],
                CONTRACT_LAST,
                preferred_element_type=jnp.float32,
            )
            if m == 0:
                gh[:, span] = value
            else:
                gh[:, span] += value
            return carry

        lax.fori_loop(0, inner // tile_f, project_back, 0)
        if m + 2 < lanes:
            fetch(2, m + 2, slot)

    def differentiate(e, carry):
        span = pl.ds(pl.multiple_of(e * count, count), count)
        weight = share_cols[span, 0:1]
        for f in range(0, inner, tile_f):
            part = slice(f, f + tile_f)
            v = gate[span, part]
            sig = jax.nn.sigmoid(v)
            slope = gh[span, part] * weight * sig
            hid[span, part] = (slope * up[span, part] * (1.0 + v * (1.0 - sig))).astype(
                jnp.bfloat16
            )
            gu[span, part] = (slope * v).astype(jnp.bfloat16)
        return carry

    lax.fori_loop(0, experts, differentiate, 0)
    sent(1)

    steps = [(g, m) for g in range(3) for m in range(lanes - 1, -1, -1)]
    for step, (g, m) in enumerate(steps):
        slot = m % 2
        fetched(0, slot, (g,))
        fetched(1, slot, (g,))
        span = slice(g * slim, (g + 1) * slim)
        value = lax.dot_general(
            hid[...], wg_buf[slot, span, :], CONTRACT_LAST, preferred_element_type=jnp.float32
        )
        value = value + lax.dot_general(
            gu[...], wu_buf[slot, span, :], CONTRACT_LAST, preferred_element_type=jnp.float32
        )
        g_buf[:, :, slim_ds(flip(i, m), g)] = value.astype(jnp.bfloat16).reshape(
            experts, count, slim
        )
        if m >= 2:
            fetch(0, m - 2, slot, (g,))
            fetch(1, m - 2, slot, (g,))
        pair_send(1, g, m)
        if step > 0:
            pair_sum(1, *steps[step - 1])
        if step == 0:
            via_sum(0, 0)
        if step == 5:
            via_sum(1, 0)
        if step == 6:
            plane_sum(0, 0)
        if step == 9:
            via_sum(1, 1)
            plane_sum(1, 0)
    pair_sum(1, 2, 0)
    via_sum(1, 2)
    plane_sum(1, 1)
    finish(0, 0)
    plane_sum(1, 2)
    finish(1, 0)
    finish(1, 1)
    finish(1, 2)
    for copies in pairs.values():
        for copy in copies:
            copy.wait_send()
    for copy in vias.values():
        copy.wait_send()
    for copy in planes.values():
        copy.wait_send()
    for copy in crossing.values():
        copy.wait_send()
    for copy in finals:
        copy.wait()


def local(sizes, tokens, routes, logits, grad_out, w_gate, w_up, w_down):
    lanes, experts, tensor = sizes
    count, width = tokens.shape
    inner = w_gate.shape[2]
    rows = count // tensor
    cols = width // lanes
    total = experts * count
    share = jax.nn.sigmoid(logits[:, 0] - logits[:, 1])
    labels = jnp.arange(experts, dtype=jnp.int32)[:, None]
    table = jnp.where(routes[None, :, 0] == labels, share[None, :], 0.0)
    table = table + jnp.where(routes[None, :, 1] == labels, 1.0 - share[None, :], 0.0)
    table = jnp.broadcast_to(table[:, None, :], (experts, 8, count))
    bf16 = jnp.bfloat16
    f32 = jnp.float32
    dma = pltpu.SemaphoreType.DMA
    result = jax.ShapeDtypeStruct((rows, width), bf16)
    anywhere = pl.BlockSpec(memory_space=pl.ANY)
    flops = 2 * total * width * inner * 6
    return pl.pallas_call(
        functools.partial(expert_kernel, sizes),
        out_shape=(result, result),
        in_specs=[anywhere] * 6,
        out_specs=(anywhere, anywhere),
        scratch_shapes=[
            pltpu.VMEM((experts, count, width), bf16),
            pltpu.VMEM((experts, count, width), bf16),
            pltpu.VMEM((2, cols, inner), bf16),
            pltpu.VMEM((2, cols, inner), bf16),
            pltpu.VMEM((2, inner, cols), bf16),
            pltpu.VMEM((total, inner), f32),
            pltpu.VMEM((total, inner), f32),
            pltpu.VMEM((total, inner), f32),
            pltpu.VMEM((total, inner), bf16),
            pltpu.VMEM((total, inner), bf16),
            pltpu.VMEM((experts, 8, count), f32),
            pltpu.VMEM((total, count), f32),
            pltpu.VMEM((2, lanes, tensor - 1, experts, rows, cols), bf16),
            pltpu.VMEM((2, 2, experts, rows, cols), bf16),
            pltpu.VMEM((2, 2, experts, rows, cols // 2), bf16),
            pltpu.VMEM((2, experts - 1, rows, cols), bf16),
            pltpu.VMEM((2, rows, cols), bf16),
            dma((3, 2, 3)),
            dma((9,)),
            dma((experts,)),
            dma((experts,)),
            dma((2, experts)),
            dma((2, experts)),
            dma((2, experts, 5)),
            dma((2, experts, 5)),
            dma((2, experts, lanes, tensor)),
            dma((2, experts, lanes, tensor)),
            dma((2, 3, lanes, tensor)),
            dma((2, 3, lanes, tensor)),
            dma((2, 3, 2, 2, experts)),
            dma((2, 3, 2, 2, experts)),
            dma((2, 3, 2, experts)),
            dma((2, 3, 2, experts)),
            dma((2, 3, experts)),
            dma((2, 3, experts)),
            dma((2, 3, lanes)),
            dma((2, 3, lanes)),
        ],
        compiler_params=pltpu.CompilerParams(
            collective_id=0, has_side_effects=True, vmem_limit_bytes=62 * 1024 * 1024
        ),
        cost_estimate=pl.CostEstimate(
            flops=flops, bytes_accessed=6 * width * inner * 2, transcendentals=2 * total * inner
        ),
        name="expert_layer",
    )(tokens, grad_out, table, w_gate[0], w_up[0], w_down[0])


def solution(mesh):
    sizes = (mesh.shape["dp"], mesh.shape["expert"], mesh.shape["tensor"])
    return jax.shard_map(
        functools.partial(local, sizes),
        mesh=mesh,
        in_specs=(
            P("expert", None),
            P("expert", None),
            P("expert", None),
            P("expert", None),
            P("expert", None, ("dp", "tensor")),
            P("expert", None, ("dp", "tensor")),
            P("expert", ("dp", "tensor"), None),
        ),
        out_specs=(P(("expert", "tensor"), None), P(("expert", "tensor"), None)),
        check_vma=False,
    )
```
